128 devices in a mesh: row: 64 (over y, z, x), rep: 2 (over core).
Axes of the slice: x: 4, y: 4, z: 4, core: 2. Of those that a mesh axis runs over, the one named last changes fastest.
Arguments:
- node_feats: bfloat16 [131072, 256], P('row')
- out_grad: bfloat16 [131072, 256], P('row'), may hold values from -6 to 6
- mask_bits: int32 [131072, 16], P('row'), may hold values from 0 to 65535
- weight: bfloat16 [256, 256], replicated, may hold values from -0.375 to 0.375
- send_rows: int32 [64, 64, 128], P('row'), may hold values from -1 to 2047, as said below
- tile_vals: bfloat16 [64, 2, 512, 128, 128], P('row', 'rep'), may hold values from -0.0625 to 0.0625
- tile_row: int32 [64, 2, 512], P('row', 'rep'), may hold values from -1 to 15, as said below
- tile_peer: int32 [64, 2, 512], P('row', 'rep'), may hold values from 0 to 63
Outputs:
- in_grad: bfloat16 [131072, 256], P('row')
- w_grad: float32 [256, 256], replicated
The draws below stay inside these ranges and needn't reach their ends.
Inputs may be any that keep to these rules, and one draw needn't show every extreme that they name: `send_rows`: empty slots (-1) follow the filled ones; the list from a block to itself is full and the list from block p to block p + 1 (cyclically) holds 32 rows. `tile_row`: empty slots (-1) follow the filled ones; a device's filled slots number 512, 256, 128 or 64, and device 0 of both axes has all 512.
All inputs are finite; a program needn't handle non-finite values.
Results may differ from the reference program's by a relative error of at most 0.0049.
Values may be sent and summed in bfloat16 or wider, within the bound.
A program may use at most 128 MiB of HBM per device.

```python
import jax
import jax.numpy as jnp
from jax import lax

F = 256
TILE = 128
ROWS_DEV = 2048
K = 512
NODES = 131072
N_ROW = 64
N_REP = 2


def tile_layout(key):
    key_a, key_b, key_c = jax.random.split(key, 3)
    level = jax.random.randint(key_a, (N_ROW, N_REP), 0, 4)
    level = level.at[0, 0].set(0)
    level = level.at[N_ROW - 1, N_REP - 1].set(1)
    live = jnp.maximum(K // jnp.left_shift(jnp.ones_like(level), level), 1)
    rows = jax.random.randint(key_b, (N_ROW, N_REP, K), 0, ROWS_DEV // TILE)
    rows = rows.at[0, 0, 0].set(ROWS_DEV // TILE - 1)
    position = jnp.arange(K, dtype=jnp.int32)
    rows = jnp.where(position[None, None, :] < live[:, :, None], rows, -1)
    peers = jax.random.randint(key_c, (N_ROW, N_REP, K), 0, N_ROW)
    peers = peers.at[0, 0, 0].set(N_ROW - 1)
    peers = peers.at[0, 0, 1].set(0)
    return (rows.astype(jnp.int32), peers.astype(jnp.int32))


def draw_tile_row(key, part):
    return tile_layout(key)[0]


def draw_tile_peer(key, part):
    return tile_layout(key)[1]


def draw_send_rows(key, part):
    key = jax.random.fold_in(key, 7)
    key_a, key_b = jax.random.split(key)
    counts = jax.random.randint(key_a, (N_ROW, N_ROW), TILE // 4, TILE + 1)
    source = jnp.arange(N_ROW, dtype=jnp.int32)
    same = source[:, None] == source[None, :]
    after = (source[:, None] + 1) % N_ROW == source[None, :]
    counts = jnp.where(after, TILE // 4, counts)
    counts = jnp.where(same, TILE, counts)
    rows = jax.random.randint(key_b, (N_ROW, N_ROW, TILE), 0, ROWS_DEV)
    slot = jnp.arange(TILE, dtype=jnp.int32)
    own = ROWS_DEV - TILE + slot
    rows = jnp.where(same[:, :, None], own[None, None, :], rows)
    rows = jnp.where(slot[None, None, :] < counts[:, :, None], rows, -1)
    return rows.astype(jnp.int32)


def draw_node_feats(key, part):
    key = jax.random.fold_in(key, 11)
    node = jnp.arange(NODES, dtype=jnp.float32)
    base = jax.random.normal(key, (NODES, F), jnp.float32)
    scale = 0.5 + 1.5 * node / NODES
    values = jnp.clip(base, -5.0, 5.0) * scale[:, None]
    return values.astype(jnp.bfloat16)


def set_ends(entries, stream_key, low, largest):
    extent = entries.shape
    place = [jax.random.randint(jax.random.fold_in(stream_key, axis), (), 0, extent[axis]) for axis in range(len(extent))]
    entries = entries.at[tuple(place)].set(low)
    longest = extent.index(max(extent))
    place[longest] = (place[longest] + 1) % extent[longest]
    return entries.at[tuple(place)].set(largest)


def shard_levels(rng, extent, shards, smallest, largest):
    gain = 1.0
    for dim, shards_of in shards:
        draws = jax.random.uniform(jax.random.fold_in(jax.random.fold_in(rng, 6), dim), (shards_of,), jnp.float32, smallest / len(shards), largest / len(shards))
        gain = gain * jnp.repeat(jnp.exp(draws), extent[dim] // shards_of).reshape((-1,) + (1,) * (len(extent) - 1 - dim))
    return gain


def bell_draw(own_key, extent, scale, most, shards=(), held_as=jnp.bfloat16):
    entries = scale * jax.random.normal(own_key, extent, jnp.float32)
    if shards:
        entries = entries * shard_levels(own_key, extent, shards, -0.22, 0.18)
    return jnp.clip(entries, -most, most).astype(held_as)


def setup_inputs(seed: int = 0) -> dict:
    key_of = jax.random.split(jax.random.key(seed), 9)
    return {
        "node_feats": draw_node_feats(jax.random.fold_in(key_of[8], 71), 0),
        "out_grad": bell_draw(key_of[1], (NODES, F), 1.0, 6.0, ((0, 64),)),
        "mask_bits": set_ends(jax.random.randint(key_of[2], (NODES, F // 16), 0, 65536), jax.random.fold_in(key_of[2], 1), 0, 65535).astype(jnp.int32),
        "weight": bell_draw(key_of[3], (F, F), F ** -0.5, 0.375),
        "send_rows": draw_send_rows(jax.random.fold_in(key_of[8], 71), 0),
        "tile_vals": bell_draw(key_of[5], (N_ROW, N_REP, K, TILE, TILE), (TILE * K * N_REP * TILE // ROWS_DEV) ** -0.5, 0.0625, ((0, 64), (1, 2))),
        "tile_row": draw_tile_row(jax.random.fold_in(key_of[8], 71), 0),
        "tile_peer": draw_tile_peer(jax.random.fold_in(key_of[8], 71), 0),
    }


def unpack_mask(mask_bits):
    shifts = jnp.arange(16, dtype=jnp.int32)
    bits = jnp.bitwise_and(jnp.right_shift(mask_bits[:, :, None], shifts[None, None, :]), 1)
    return bits.reshape(mask_bits.shape[0], mask_bits.shape[1] * 16)


def reference(node_feats, out_grad, mask_bits, weight, send_rows, tile_vals, tile_row, tile_peer):
    mask = unpack_mask(mask_bits)
    grad_pre = jnp.where(mask == 1, out_grad, jnp.zeros_like(out_grad)).astype(jnp.bfloat16)
    blocks = grad_pre.reshape(N_ROW, ROWS_DEV, F)
    row_tiles = ROWS_DEV // TILE

    def one_block(q):
        listed = send_rows[:, q, :]
        safe = jnp.clip(listed, 0, ROWS_DEV - 1).astype(jnp.int32)
        got = jnp.take_along_axis(blocks, safe[:, :, None], axis=1)
        got = jnp.where(listed[:, :, None] >= 0, got, jnp.zeros_like(got))
        values = tile_vals[q].reshape(N_REP * K, TILE, TILE).astype(jnp.float32)
        rows = tile_row[q].reshape(N_REP * K)
        peers = tile_peer[q].reshape(N_REP * K)
        sources = got[peers].astype(jnp.float32)
        prods = jnp.einsum('kab,kbf->kaf', values, sources)
        prods = jnp.where(rows[:, None, None] >= 0, prods, jnp.zeros_like(prods))
        target = jnp.clip(rows, 0, row_tiles - 1).astype(jnp.int32)
        total = jnp.zeros((row_tiles, TILE, F), jnp.float32).at[target].add(prods)
        return total.reshape(ROWS_DEV, F)

    agg = lax.map(one_block, jnp.arange(N_ROW, dtype=jnp.int32))
    agg = agg.reshape(NODES, F).astype(jnp.bfloat16)
    in_grad = lax.dot_general(agg, weight, (((1,), (1,)), ((), ())), preferred_element_type=jnp.float32).astype(jnp.bfloat16)
    w_sum = lax.dot_general(node_feats, agg, (((0,), (0,)), ((), ())), preferred_element_type=jnp.float32)
    w_grad = w_sum * jnp.float32(1.0 / (NODES ** 0.5))
    return in_grad, w_grad
```

```python
import functools
import math

import jax
import jax.numpy as jnp
from jax import lax
from jax.experimental import pallas as pl
from jax.experimental.pallas import tpu as pltpu
from jax.sharding import PartitionSpec as P

MESH = pl.DeviceIdType.MESH
SIDE = 4
UORDER = (0, 7, 1, 6, 2, 5, 3, 4)


def place(me):
    return me % SIDE, me // (SIDE * SIDE), (me // SIDE) % SIDE


def shifted(me, off, sign):
    x, y, z = place(me)
    dx, dy, dz = off
    return (
        ((y + sign * dy + SIDE) % SIDE) * SIDE + (z + sign * dz + SIDE) % SIDE
    ) * SIDE + (x + sign * dx + SIDE) % SIDE


def offset_of(i, u):
    g, w = 7 - i, UORDER[u]
    return (
        g % 2 + 2 * (w & 1),
        (g // 2) % 2 + 2 * ((w >> 1) & 1),
        g // 4 + 2 * (w >> 2),
    )


def front_kernel(
    og_ref, mb_ref, sr_ref, recv_ref,
    gp, listed, turned, wide, hot, sbuf,
    ssem, rsem, fssem, frsem, own_sem,
):
    me = lax.axis_index("row")
    core = lax.axis_index("rep")
    rows, width = gp.shape
    half = sbuf.shape[1]
    tile = 2 * half

    barrier = pltpu.get_barrier_semaphore()
    pl.semaphore_signal(barrier, inc=1, device_id=(me, 1 - core), device_id_type=MESH)

    @pl.loop(1, 64)
    def _(j):
        q = shifted(me, (j % 4, (j // 4) % 4, j // 16), 1)
        pl.semaphore_signal(barrier, inc=1, device_id=(q, core), device_id_type=MESH)

    words = mb_ref.shape[1]
    feature = lax.broadcasted_iota(jnp.int32, (words, width), 1)
    word = lax.broadcasted_iota(jnp.int32, (words, width), 0)
    here = feature // 16 == word
    low = jnp.where(here & (feature % 16 < 8), 1.0, 0.0).astype(jnp.bfloat16)
    high = jnp.where(here & (feature % 16 >= 8), 1.0, 0.0).astype(jnp.bfloat16)
    step = 256
    bit = lax.broadcasted_iota(jnp.int32, (step, width), 1) % 8

    @pl.loop(0, rows // step)
    def _(b):
        at = pl.ds(pl.multiple_of(b * step, step), step)
        bits = mb_ref[at, :]
        lo = (bits & 255).astype(jnp.float32).astype(jnp.bfloat16)
        hi = (bits >> 8).astype(jnp.float32).astype(jnp.bfloat16)
        byte = jnp.dot(lo, low, preferred_element_type=jnp.float32)
        byte += jnp.dot(hi, high, preferred_element_type=jnp.float32)
        keep = (byte.astype(jnp.int32) >> bit) & 1
        grad = og_ref[at, :].astype(jnp.float32)
        gp[at, :] = jnp.where(keep == 1, grad, 0.0).astype(jnp.bfloat16)

    listed[...] = jnp.full(listed.shape, -1, jnp.int32)
    for u in range(8):

        @pl.loop(0, 8)
        def _(i, u=u):
            q = shifted(me, offset_of(i, u), 1)
            listed[pl.ds(i * 8 + u, 1), :] = sr_ref[pl.ds(q, 1), :]

    turned[...] = listed[...].T
    mine = turned[pl.ds(pl.multiple_of(core * half, half), half), :]
    for j in range(64):
        wide[j] = jnp.broadcast_to(mine[:, j : j + 1], (half, 128))

    lane = lax.broadcasted_iota(jnp.int32, (half, 128), 1)
    halves = pl.ds(pl.multiple_of(core * half, half), half)

    def send(i, u):
        q = shifted(me, offset_of(i, u), 1)
        j = i * 8 + u
        return pltpu.make_async_remote_copy(
            src_ref=sbuf.at[j], dst_ref=recv_ref.at[me, halves],
            send_sem=ssem.at[j], recv_sem=rsem.at[j],
            device_id=(q, core), device_id_type=MESH,
        )

    def forward(i, u):
        p = shifted(me, offset_of(i, u), -1)
        j = i * 8 + u
        return pltpu.make_async_remote_copy(
            src_ref=recv_ref.at[p, halves], dst_ref=recv_ref.at[p, halves],
            send_sem=fssem.at[j], recv_sem=frsem.at[j],
            device_id=(me, 1 - core), device_id_type=MESH,
        )

    def keep_own():
        return pltpu.make_async_copy(sbuf.at[56], recv_ref.at[me, halves], own_sem)

    @pl.loop(0, 8)
    def _(i):
        for u in range(8):
            listed_at = wide[i * 8 + u]
            block = listed_at >> 7
            one = jnp.where((listed_at & 127) == lane, 1.0, 0.0)
            for t in range(rows // 128):
                hot[u * half : (u + 1) * half, t * 128 : (t + 1) * 128] = jnp.where(
                    block == t, one, 0.0
                ).astype(jnp.bfloat16)
        picked = jnp.dot(hot[...], gp[...], preferred_element_type=jnp.float32)
        for u in range(8):
            sbuf[i * 8 + u] = picked[u * half : (u + 1) * half].astype(jnp.bfloat16)

        @pl.when(i == 0)
        def _():
            pl.semaphore_wait(barrier, 64)

        for u in range(8):
            if u == 0:

                @pl.when(i < 7)
                def _(u=u):
                    send(i, u).start()

                @pl.when(i == 7)
                def _():
                    keep_own().start()
            else:
                send(i, u).start()

    @pl.loop(0, 8)
    def _(i):
        for u in range(8):
            if u == 0:

                @pl.when(i < 7)
                def _(u=u):
                    send(i, u).wait_recv()

                @pl.when(i == 7)
                def _():
                    keep_own().wait()
            else:
                send(i, u).wait_recv()
            forward(i, u).start()

    @pl.loop(0, 8)
    def _(i):
        for u in range(8):
            if u == 0:

                @pl.when(i < 7)
                def _(u=u):
                    send(i, u).wait_send()
            else:
                send(i, u).wait_send()
            forward(i, u).wait()


def front(out_grad, mask_bits, listed):
    rows, width = out_grad.shape
    peers, tile = listed.shape
    half = tile // 2
    vmem = pl.BlockSpec(memory_space=pltpu.VMEM)
    return pl.pallas_call(
        front_kernel,
        out_shape=jax.ShapeDtypeStruct((peers, tile, width), jnp.bfloat16),
        in_specs=[vmem, vmem, vmem],
        out_specs=pl.BlockSpec(memory_space=pl.ANY),
        scratch_shapes=[
            pltpu.VMEM((rows, width), jnp.bfloat16),
            pltpu.VMEM((128, 128), jnp.int32),
            pltpu.VMEM((128, 128), jnp.int32),
            pltpu.VMEM((peers, half, 128), jnp.int32),
            pltpu.VMEM((8 * half, rows), jnp.bfloat16),
            pltpu.VMEM((peers, half, width), jnp.bfloat16),
            pltpu.SemaphoreType.DMA((peers,)),
            pltpu.SemaphoreType.DMA((peers,)),
            pltpu.SemaphoreType.DMA((peers,)),
            pltpu.SemaphoreType.DMA((peers,)),
            pltpu.SemaphoreType.DMA,
        ],
        compiler_params=pltpu.CompilerParams(
            collective_id=0, has_side_effects=True, vmem_limit_bytes=32 * 2**20
        ),
        name="front",
    )(out_grad, mask_bits, listed)


def local(node_feats, out_grad, mask_bits, weight, send_rows, tile_vals, tile_row, tile_peer):
    rows_here = node_feats.shape[0]
    width = node_feats.shape[1]
    received = front(out_grad, mask_bits, send_rows[0])
    values = tile_vals[0, 0]
    rows = tile_row[0, 0]
    peers = tile_peer[0, 0]
    slots = values.shape[0]
    tile = values.shape[1]
    block = min(32, slots)
    row_tiles = rows_here // tile
    sources_all = received.shape[0]
    flat_received = received.reshape(sources_all, tile * width)
    peer_ids = jnp.arange(sources_all, dtype=jnp.int32)
    tile_ids = jnp.arange(row_tiles, dtype=jnp.int32)
    live_count = jnp.sum((rows >= 0).astype(jnp.int32))
    block_count = (live_count + block - 1) // block

    def add_block(index, total):
        block_vals = lax.dynamic_slice_in_dim(values, index * block, block, 0)
        block_rows = lax.dynamic_slice_in_dim(rows, index * block, block, 0)
        block_peers = lax.dynamic_slice_in_dim(peers, index * block, block, 0)
        peer_hot = (block_peers[:, None] == peer_ids[None, :]).astype(jnp.bfloat16)
        sources = jnp.dot(peer_hot, flat_received, preferred_element_type=jnp.float32)
        sources = sources.astype(jnp.bfloat16).reshape(block, tile, width)
        prods = jnp.einsum("kab,kbf->kaf", block_vals, sources, preferred_element_type=jnp.float32)
        row_hot = (tile_ids[:, None] == block_rows[None, :]).astype(jnp.float32)
        added = jnp.dot(
            row_hot,
            prods.reshape(block, tile * width),
            precision=lax.Precision.HIGHEST,
            preferred_element_type=jnp.float32,
        )
        return total + added

    start = jnp.zeros((row_tiles, tile * width), jnp.float32)
    partial_value = lax.fori_loop(0, block_count, add_block, start).reshape(rows_here, width)
    scale = 1.0 / math.sqrt(rows_here * lax.axis_size("row"))
    agg = lax.psum(partial_value, "rep").astype(jnp.bfloat16)
    in_grad = lax.dot_general(
        agg, weight, (((1,), (1,)), ((), ())), preferred_element_type=jnp.float32
    ).astype(jnp.bfloat16)
    w_term = lax.dot_general(
        node_feats, agg, (((0,), (0,)), ((), ())), preferred_element_type=jnp.float32
    )
    w_sum = lax.psum(w_term, "row")
    w_grad = w_sum * jnp.float32(scale)
    return (in_grad, w_grad)


def solution(mesh):
    placed = (
        P("row", None),
        P("row", None),
        P("row", None),
        P(),
        P("row", None, None),
        P("row", "rep", None, None, None),
        P("row", "rep", None),
        P("row", "rep", None),
    )
    return jax.shard_map(
        local, mesh=mesh, in_specs=placed, out_specs=(P("row", None), P()), check_vma=False
    )
```

```python
import math

import jax
import jax.numpy as jnp
from jax import lax
from jax.experimental import pallas as pl
from jax.experimental.pallas import tpu as pltpu
from jax.sharding import PartitionSpec as P

MESH = pl.DeviceIdType.MESH
SIDE = 4
UORDER = (0, 7, 1, 6, 2, 5, 3, 4)
GROUP = 4
UNROLL = 20
PLANE = [(0, a, b) for a in range(4) for b in range(4) if (a, b) != (0, 0)]
LINE = [(a, 0, 0) for a in range(1, 4)]


def place(me):
    return me % SIDE, me // (SIDE * SIDE), (me // SIDE) % SIDE


def shifted(me, off, sign):
    x, y, z = place(me)
    dx, dy, dz = off
    return (
        ((y + sign * dy + SIDE) % SIDE) * SIDE + (z + sign * dz + SIDE) % SIDE
    ) * SIDE + (x + sign * dx + SIDE) % SIDE


def offset_of(i, u):
    g, w = 7 - i, UORDER[u]
    return (
        g % 2 + 2 * (w & 1),
        (g // 2) % 2 + 2 * ((w >> 1) & 1),
        g // 4 + 2 * (w >> 2),
    )


def iota(shape, dim):
    return lax.broadcasted_iota(jnp.int32, shape, dim)


def layout_tables(row, peer, row_tiles, zero_peer, places):
    slots = row.shape[1]
    key = jnp.where(row < 0, row_tiles, row)
    key_down = jnp.broadcast_to(key, (128, slots)).T
    peer_down = jnp.broadcast_to(peer, (128, slots)).T
    down = iota((slots, 128), 0)
    across = iota((slots, 128), 1)
    count = jnp.sum((key_down == across).astype(jnp.int32), axis=0, keepdims=True)
    groups = jnp.where(iota((1, 128), 1) < row_tiles, (count + GROUP - 1) // GROUP, 0)
    groups_down = jnp.broadcast_to(groups, (128, 128)).T
    r_down, r_across = iota((128, 128), 0), iota((128, 128), 1)
    first = jnp.sum(jnp.where(r_down < r_across, groups_down, 0), axis=0, keepdims=True)
    first_down = jnp.broadcast_to(first, (128, 128)).T

    spots = []
    for b in range(slots // 128):
        key_here = key[:, b * 128 : (b + 1) * 128]
        before = (key_down == key_here) & (down < across + b * 128)
        rank = jnp.sum(before.astype(jnp.int32), axis=0, keepdims=True)
        base = jnp.sum(jnp.where(r_down < key_here, groups_down, 0), axis=0, keepdims=True)
        spots.append(jnp.where(key_here < row_tiles, base * GROUP + rank, -1))
    spot_down = jnp.broadcast_to(jnp.concatenate(spots, axis=1), (128, slots)).T

    slot_at, peer_at, goes_on = [], [], []
    for b in range(places // 128):
        hit = spot_down == across + b * 128
        slot_at.append(jnp.sum(jnp.where(hit, down, 0), axis=0, keepdims=True))
        peer_at.append(
            jnp.sum(jnp.where(hit, peer_down - zero_peer, 0), axis=0, keepdims=True) + zero_peer
        )
        opens = (first_down == r_across + b * 128) & (groups_down > 0)
        goes_on.append(1 - jnp.sum(opens.astype(jnp.int32), axis=0, keepdims=True))
    last = jnp.where(groups > 0, first + groups, 0)
    last = jnp.concatenate([last, jnp.zeros((1, places - 128), jnp.int32)], axis=1)
    rows = [jnp.concatenate(part, axis=1) for part in (slot_at, peer_at, goes_on)] + [last]
    return jnp.concatenate(rows + [jnp.zeros((8 - len(rows), places), jnp.int32)], axis=0)


def kernel(
    scale,
    og_hbm, mb_hbm, sr_hbm, row_hbm, peer_hbm, nf_hbm, wt_hbm, tv_hbm,
    ing_hbm, wg_hbm,
    og, mb, sr, row_v, peer_v, nf, wt, tv,
    gp, listed, turned, wide, hot, sbuf, recv, table_v, table_s,
    steps, part, other, nft, ing, agg, term, red, line, done,
    in_sem, tv_sem, table_sem, own_sem, out_sem,
    ssem, rsem, fssem, frsem, pssem, prsem, r1s, r1r, r2s, r2r, r3s, r3r,
):
    me = lax.axis_index("row")
    core = lax.axis_index("rep")
    rows, width = gp.shape
    peers, half = sbuf.shape[:2]
    tile = 2 * half
    row_tiles = rows // tile
    sib = (me, 1 - core)

    loads = [
        pltpu.make_async_copy(src, dst, in_sem.at[n])
        for n, (src, dst) in enumerate(
            (
                (sr_hbm, sr), (mb_hbm, mb), (og_hbm, og), (row_hbm, row_v),
                (peer_hbm, peer_v), (nf_hbm, nf), (wt_hbm, wt),
            )
        )
    ]
    for load in loads[:5]:
        load.start()

    barrier = pltpu.get_barrier_semaphore()
    pl.semaphore_signal(barrier, inc=1, device_id=sib, device_id_type=MESH)

    @pl.loop(1, 64)
    def _(j):
        q = shifted(me, (j % 4, (j // 4) % 4, j // 16), 1)
        pl.semaphore_signal(barrier, inc=1, device_id=(q, core), device_id_type=MESH)

    for off in PLANE:
        q = shifted(me, off, 1)
        pl.semaphore_signal(barrier, inc=1, device_id=(q, 1 - core), device_id_type=MESH)
    greeted = 1 + 63 + len(PLANE)

    loads[0].wait()
    listed[...] = jnp.full(listed.shape, -1, jnp.int32)
    for u in range(8):

        @pl.loop(0, 8)
        def _(i, u=u):
            q = shifted(me, offset_of(i, u), 1)
            listed[pl.ds(i * 8 + u, 1), :] = sr[pl.ds(q, 1), :]

    turned[...] = listed[...].T
    mine = turned[pl.ds(pl.multiple_of(core * half, half), half), :]
    for j in range(64):
        wide[j] = jnp.broadcast_to(mine[:, j : j + 1], (half, 128))

    words = mb.shape[0]
    feature = iota((2 * words, width), 1)
    byte_at = iota((2 * words, width), 0)
    spread = (feature // 16 == byte_at % words) & ((feature % 16 >= 8) == (byte_at >= words))
    spread = jnp.where(spread, 1.0, 0.0).astype(jnp.bfloat16)
    step = 256
    bit = iota((step, width), 1) % 8
    loads[1].wait()
    loads[2].wait()

    @pl.loop(0, rows // step)
    def _(b):
        at = pl.ds(pl.multiple_of(b * step, step), step)
        bits = mb[:, at]
        both = jnp.concatenate([bits & 255, bits >> 8], axis=0)
        both = both.astype(jnp.float32).astype(jnp.bfloat16)
        byte = lax.dot_general(
            both, spread, (((0,), (0,)), ((), ())), preferred_element_type=jnp.float32
        )
        keep = (byte.astype(jnp.int32) >> bit) & 1
        grad = og[at, :].astype(jnp.float32)
        gp[at, :] = jnp.where(keep == 1, grad, 0.0).astype(jnp.bfloat16)

    lane = iota((half, 128), 1)
    halves = pl.ds(pl.multiple_of(core * half, half), half)

    def send(i, u):
        q = shifted(me, offset_of(i, u), 1)
        j = i * 8 + u
        return pltpu.make_async_remote_copy(
            src_ref=sbuf.at[j], dst_ref=recv.at[me, halves],
            send_sem=ssem.at[j], recv_sem=rsem.at[j],
            device_id=(q, core), device_id_type=MESH,
        )

    def forward(i, u):
        p = shifted(me, offset_of(i, u), -1)
        j = i * 8 + u
        return pltpu.make_async_remote_copy(
            src_ref=recv.at[p, halves], dst_ref=recv.at[p, halves],
            send_sem=fssem.at[j], recv_sem=frsem.at[j],
            device_id=sib, device_id_type=MESH,
        )

    def keep_own():
        return pltpu.make_async_copy(sbuf.at[peers - 8], recv.at[me, halves], own_sem)

    @pl.loop(0, 8)
    def _(i):
        for u in range(8):
            listed_at = wide[i * 8 + u]
            block = listed_at >> 7
            one = jnp.where((listed_at & 127) == lane, 1.0, 0.0)
            for t in range(rows // 128):
                hot[u * half : (u + 1) * half, t * 128 : (t + 1) * 128] = jnp.where(
                    block == t, one, 0.0
                ).astype(jnp.bfloat16)
        picked = jnp.dot(hot[...], gp[...], preferred_element_type=jnp.float32)
        for u in range(8):
            sbuf[i * 8 + u] = picked[u * half : (u + 1) * half].astype(jnp.bfloat16)

        @pl.when(i == 0)
        def _():
            pl.semaphore_wait(barrier, greeted)

        for u in range(8):
            if u == 0:

                @pl.when(i < 7)
                def _(u=u):
                    send(i, u).start()

                @pl.when(i == 7)
                def _():
                    keep_own().start()
            else:
                send(i, u).start()

    fill = pltpu.make_async_copy(tv_hbm, tv, tv_sem)
    fill.start()
    for load in loads[5:]:
        load.start()
    loads[3].wait()
    loads[4].wait()
    table_v[...] = layout_tables(
        row_v[...], peer_v[...], row_tiles, peers, table_v.shape[1]
    )
    table_copy = pltpu.make_async_copy(table_v, table_s, table_sem)
    table_copy.start()
    recv[peers] = jnp.zeros(recv.shape[1:], recv.dtype)
    steps[0] = jnp.zeros(steps.shape[1:], steps.dtype)
    loads[5].wait()
    loads[6].wait()
    columns = pl.ds(pl.multiple_of(core * 128, 128), 128)

    @pl.loop(0, row_tiles)
    def _(r):
        at = pl.ds(pl.multiple_of(r * tile, tile), tile)
        nft[r] = nf[at, columns].T

    table_copy.wait()

    @pl.loop(0, 8)
    def _(i):
        for u in range(8):
            if u == 0:

                @pl.when(i < 7)
                def _(u=u):
                    send(i, u).wait_recv()

                @pl.when(i == 7)
                def _():
                    keep_own().wait()
            else:
                send(i, u).wait_recv()
            forward(i, u).start()

    @pl.loop(0, 8)
    def _(i):
        for u in range(8):
            if u == 0:

                @pl.when(i < 7)
                def _(u=u):
                    send(i, u).wait_send()
            else:
                send(i, u).wait_send()
            forward(i, u).wait()

    fill.wait()

    @pl.loop(0, (steps.shape[0] - 1) // UNROLL)
    def _(i):
        for u in range(UNROLL):
            g = i * UNROLL + u
            left = jnp.concatenate([tv[table_s[0, GROUP * g + v]] for v in range(GROUP)], axis=1)
            right = jnp.concatenate([recv[table_s[1, GROUP * g + v]] for v in range(GROUP)], axis=0)
            prod = jnp.dot(left, right, preferred_element_type=jnp.float32)
            steps[g + 1] = jnp.where(table_s[2, g] == 1, steps[g], 0.0) + prod

    def swap(r):
        return pltpu.make_async_remote_copy(
            src_ref=part.at[r], dst_ref=other.at[r],
            send_sem=pssem.at[r], recv_sem=prsem.at[r],
            device_id=sib, device_id_type=MESH,
        )

    for r in range(row_tiles):
        part[r] = steps[table_s[3, r]]
        swap(r).start()
    term[...] = jnp.zeros(term.shape, term.dtype)
    for b in range(row_tiles // GROUP):
        for r in range(b * GROUP, (b + 1) * GROUP):
            swap(r).wait()
            agg[r * tile : (r + 1) * tile, :] = (part[r] + other[r]).astype(jnp.bfloat16)
        at = slice(b * GROUP * tile, (b + 1) * GROUP * tile)
        left = jnp.concatenate([nft[b * GROUP + v] for v in range(GROUP)], axis=1)
        term[...] += jnp.dot(left, agg[at, :], preferred_element_type=jnp.float32)

    x, y, z = place(me)
    spot = y * SIDE + z
    piece = red.shape[1]

    def rows_of(s):
        return pl.ds(pl.multiple_of(s * piece, piece), piece)

    def first_send(n):
        q = shifted(me, PLANE[n], 1)
        return pltpu.make_async_remote_copy(
            src_ref=term.at[rows_of(q // SIDE)], dst_ref=red.at[n],
            send_sem=r1s.at[n], recv_sem=r1r.at[n],
            device_id=(q, core), device_id_type=MESH,
        )

    def second_send(n):
        return pltpu.make_async_remote_copy(
            src_ref=line.at[x], dst_ref=line.at[x],
            send_sem=r2s.at[n], recv_sem=r2r.at[n],
            device_id=(shifted(me, LINE[n], 1), core), device_id_type=MESH,
        )

    def third_send(n):
        if n < 2 * len(PLANE):
            to = (shifted(me, PLANE[n // 2], 1), core if n % 2 == 0 else 1 - core)
        else:
            to = sib
        at = pl.ds(pl.multiple_of(core * 128 + spot * piece, piece), piece)
        return pltpu.make_async_remote_copy(
            src_ref=done.at[at], dst_ref=done.at[at],
            send_sem=r3s.at[n], recv_sem=r3r.at[n],
            device_id=to, device_id_type=MESH,
        )

    for n in range(len(PLANE)):
        first_send(n).start()

    @pl.loop(0, rows // 512)
    def _(b):
        at = pl.ds(pl.multiple_of(b * 512, 512), 512)
        ing[at, :] = lax.dot_general(
            agg[at, :], wt[...], (((1,), (1,)), ((), ())), preferred_element_type=jnp.float32
        ).astype(jnp.bfloat16)

    out_copy = pltpu.make_async_copy(ing, ing_hbm, out_sem.at[0])
    out_copy.start()
    mine_sum = term[rows_of(spot), :]
    for n in range(len(PLANE)):
        first_send(n).wait_recv()
        mine_sum += red[n]
    line[x] = mine_sum
    for n in range(len(LINE)):
        second_send(n).start()
    for n in range(len(LINE)):
        second_send(n).wait_recv()
    total = ((line[0] + line[1]) + line[2]) + line[3]
    done[pl.ds(pl.multiple_of(core * 128 + spot * piece, piece), piece), :] = total * jnp.float32(scale)
    thirds = 2 * len(PLANE) + 1
    for n in range(thirds):
        third_send(n).start()
    for n in range(thirds):
        third_send(n).wait_recv()
    w_copy = pltpu.make_async_copy(done, wg_hbm, out_sem.at[1])
    w_copy.start()
    for n in range(len(PLANE)):
        first_send(n).wait_send()
    for n in range(len(LINE)):
        second_send(n).wait_send()
    for n in range(thirds):
        third_send(n).wait_send()
    out_copy.wait()
    w_copy.wait()


def local(node_feats, out_grad, mask_bits, weight, send_rows, tile_vals, tile_row, tile_peer):
    rows, width = node_feats.shape
    peers, tile = send_rows.shape[1:]
    slots = tile_vals.shape[2]
    half = tile // 2
    row_tiles = rows // tile
    words = mask_bits.shape[1]
    most = -(-(slots + row_tiles * (GROUP - 1)) // GROUP)
    most = -(-most // UNROLL) * UNROLL
    places = -(-most * GROUP // 128) * 128
    piece = width // 2 // 16
    scale = 1.0 / math.sqrt(rows * lax.axis_size("row"))
    anywhere = pl.BlockSpec(memory_space=pl.ANY)
    bf16, f32, i32 = jnp.bfloat16, jnp.float32, jnp.int32
    dma = pltpu.SemaphoreType.DMA
    thirds = 2 * len(PLANE) + 1
    return pl.pallas_call(
        lambda *refs: kernel(scale, *refs),
        out_shape=(
            jax.ShapeDtypeStruct((rows, width), bf16),
            jax.ShapeDtypeStruct((width, width), f32),
        ),
        in_specs=[anywhere] * 8,
        out_specs=(anywhere, anywhere),
        scratch_shapes=[
            pltpu.VMEM((rows, width), bf16),
            pltpu.VMEM((words, rows), i32),
            pltpu.VMEM((peers, tile), i32),
            pltpu.VMEM((1, slots), i32),
            pltpu.VMEM((1, slots), i32),
            pltpu.VMEM((rows, width), bf16),
            pltpu.VMEM((width, width), bf16),
            pltpu.VMEM((slots, tile, tile), bf16),
            pltpu.VMEM((rows, width), bf16),
            pltpu.VMEM((128, 128), i32),
            pltpu.VMEM((128, 128), i32),
            pltpu.VMEM((peers, half, 128), i32),
            pltpu.VMEM((8 * half, rows), bf16),
            pltpu.VMEM((peers, half, width), bf16),
            pltpu.VMEM((peers + 1, tile, width), bf16),
            pltpu.VMEM((8, places), i32),
            pltpu.SMEM((8, places), i32),
            pltpu.VMEM((most + 1, tile, width), f32),
            pltpu.VMEM((row_tiles, tile, width), f32),
            pltpu.VMEM((row_tiles, tile, width), f32),
            pltpu.VMEM((row_tiles, width // 2, tile), bf16),
            pltpu.VMEM((rows, width), bf16),
            pltpu.VMEM((rows, width), bf16),
            pltpu.VMEM((width // 2, width), f32),
            pltpu.VMEM((len(PLANE), piece, width), f32),
            pltpu.VMEM((SIDE, piece, width), f32),
            pltpu.VMEM((width, width), f32),
            dma((7,)), dma, dma, dma, dma((2,)),
            dma((peers,)), dma((peers,)), dma((peers,)), dma((peers,)),
            dma((row_tiles,)), dma((row_tiles,)),
            dma((len(PLANE),)), dma((len(PLANE),)),
            dma((len(LINE),)), dma((len(LINE),)),
            dma((thirds,)), dma((thirds,)),
        ],
        compiler_params=pltpu.CompilerParams(
            collective_id=0, has_side_effects=True, vmem_limit_bytes=60 * 2**20
        ),
        name="layer",
    )(
        out_grad, mask_bits.T, send_rows[0], tile_row[0], tile_peer[0],
        node_feats, weight, tile_vals[0, 0],
    )


def solution(mesh):
    placed = (
        P("row", None),
        P("row", None),
        P("row", None),
        P(),
        P("row", None, None),
        P("row", "rep", None, None, None),
        P("row", "rep", None),
        P("row", "rep", None),
    )
    return jax.shard_map(
        local, mesh=mesh, in_specs=placed, out_specs=(P("row", None), P()), check_vma=False
    )
```

```python
import math

import jax
import jax.numpy as jnp
from jax import lax
from jax.experimental import pallas as pl
from jax.experimental.pallas import tpu as pltpu
from jax.sharding import PartitionSpec as P

MESH = pl.DeviceIdType.MESH
SIDE = 4
UORDER = (0, 7, 1, 6, 2, 5, 3, 4)
GROUP = 4
UNROLL = 20
BATCH = 4
PLANE = [(0, a, b) for a in range(4) for b in range(4) if (a, b) != (0, 0)]
LINE = [(a, 0, 0) for a in range(1, 4)]


def ring(v):
    return [v] + [lax.rem(v + d, SIDE) for d in range(1, SIDE)]


def group_rows(i, x, y, z, sign):
    g = 7 - i
    odd = (lax.rem(g, 2), lax.rem(lax.div(g, 2), 2), lax.div(g, 4))
    at = [
        [lax.rem(v + sign * o + SIDE, SIDE), lax.rem(v + sign * o + SIDE + 2, SIDE)]
        for v, o in zip((x, y, z), odd)
    ]
    return [
        at[1][(w >> 1) & 1] * (SIDE * SIDE) + at[2][w >> 2] * SIDE + at[0][w & 1] for w in UORDER
    ]


def iota(shape, dim):
    return lax.broadcasted_iota(jnp.int32, shape, dim)


def layout_tables(row, peer, row_tiles, zero_peer, places):
    slots = row.shape[1]
    key = jnp.where(row < 0, row_tiles, row)
    key_down = jnp.broadcast_to(key, (128, slots)).T
    peer_down = jnp.broadcast_to(peer, (128, slots)).T
    down = iota((slots, 128), 0)
    across = iota((slots, 128), 1)
    count = jnp.sum((key_down == across).astype(jnp.int32), axis=0, keepdims=True)
    groups = jnp.where(iota((1, 128), 1) < row_tiles, (count + GROUP - 1) // GROUP, 0)
    groups_down = jnp.broadcast_to(groups, (128, 128)).T
    r_down, r_across = iota((128, 128), 0), iota((128, 128), 1)
    first = jnp.sum(jnp.where(r_down < r_across, groups_down, 0), axis=0, keepdims=True)
    first_down = jnp.broadcast_to(first, (128, 128)).T

    spots = []
    for b in range(slots // 128):
        key_here = key[:, b * 128 : (b + 1) * 128]
        before = (key_down == key_here) & (down < across + b * 128)
        rank = jnp.sum(before.astype(jnp.int32), axis=0, keepdims=True)
        base = jnp.sum(jnp.where(r_down < key_here, groups_down, 0), axis=0, keepdims=True)
        spots.append(jnp.where(key_here < row_tiles, base * GROUP + rank, -1))
    spot_down = jnp.broadcast_to(jnp.concatenate(spots, axis=1), (128, slots)).T

    slot_at, peer_at, goes_on = [], [], []
    for b in range(places // 128):
        hit = spot_down == across + b * 128
        slot_at.append(jnp.sum(jnp.where(hit, down, 0), axis=0, keepdims=True))
        peer_at.append(
            jnp.sum(jnp.where(hit, peer_down - zero_peer, 0), axis=0, keepdims=True) + zero_peer
        )
        opens = (first_down == r_across + b * 128) & (groups_down > 0)
        goes_on.append(1 - jnp.sum(opens.astype(jnp.int32), axis=0, keepdims=True))
    last = jnp.where(groups > 0, first + groups, 0)
    last = jnp.concatenate([last, jnp.zeros((1, places - 128), jnp.int32)], axis=1)
    rows = [jnp.concatenate(part, axis=1) for part in (slot_at, peer_at, goes_on)] + [last]
    return jnp.concatenate(rows + [jnp.zeros((8 - len(rows), places), jnp.int32)], axis=0)


def kernel(
    scale,
    og_hbm, mb_hbm, sr_hbm, row_hbm, peer_hbm, nf_hbm, wt_hbm, tv_hbm,
    ing_hbm, wg_hbm,
    og, mb, sr, row_v, peer_v, nf, wt, tv,
    gp, listed, turned, wide, hot, sbuf, recv, table_v, table_s,
    steps, part, other, nft, ing, agg, term, red, line, done,
    in_sem, tv_sem, table_sem, own_sem, out_sem,
    near_sem, ssem, rsem, fssem, frsem, pssem, prsem, r1s, r1r, r2s, r2r, r3s, r3r, r4s, r4r,
):
    me = lax.axis_index("row")
    core = lax.axis_index("rep")
    x, z, y = lax.rem(me, SIDE), lax.rem(lax.div(me, SIDE), SIDE), lax.div(me, SIDE * SIDE)
    xs, ys, zs = ring(x), ring(y), ring(z)

    def shifted(off):
        return ys[off[1]] * (SIDE * SIDE) + zs[off[2]] * SIDE + xs[off[0]]

    rows, width = gp.shape
    peers, half = sbuf.shape[:2]
    tile = 2 * half
    row_tiles = rows // tile
    sib = (me, 1 - core)

    loads = [
        pltpu.make_async_copy(src, dst, in_sem.at[n])
        for n, (src, dst) in enumerate(
            (
                (sr_hbm, sr), (mb_hbm, mb), (og_hbm, og), (row_hbm, row_v),
                (peer_hbm, peer_v), (nf_hbm, nf), (wt_hbm, wt),
            )
        )
    ]
    for load in loads[:5]:
        load.start()

    barrier = pltpu.get_barrier_semaphore()
    pl.semaphore_signal(barrier, inc=1, device_id=sib, device_id_type=MESH)
    for off in LINE + PLANE:
        pl.semaphore_signal(
            barrier, inc=1, device_id=(shifted(off), core), device_id_type=MESH
        )
    greeted = 1 + len(LINE) + len(PLANE)

    loads[0].wait()
    listed[...] = jnp.full(listed.shape, -1, jnp.int32)

    @pl.loop(0, 8)
    def _(i):
        for u, q in enumerate(group_rows(i, x, y, z, 1)):
            listed[pl.ds(i * 8 + u, 1), :] = sr[pl.ds(q, 1), :]

    turned[...] = listed[...].T
    mine = turned[pl.ds(pl.multiple_of(core * half, half), half), :]
    for j in range(64):
        wide[j] = jnp.broadcast_to(mine[:, j : j + 1], (half, 128))

    pl.semaphore_wait(barrier, greeted)
    for off in LINE:
        pl.semaphore_signal(
            near_sem, inc=1, device_id=(shifted(off), core), device_id_type=MESH
        )

    words = mb.shape[0]
    feature = iota((2 * words, width), 1)
    byte_at = iota((2 * words, width), 0)
    spread = (feature // 16 == byte_at % words) & ((feature % 16 >= 8) == (byte_at >= words))
    spread = jnp.where(spread, 1.0, 0.0).astype(jnp.bfloat16)
    step = 256
    bit = iota((step, width), 1) % 8
    loads[1].wait()
    loads[2].wait()

    @pl.loop(0, rows // step)
    def _(b):
        at = pl.ds(pl.multiple_of(b * step, step), step)
        bits = mb[:, at]
        both = jnp.concatenate([bits & 255, bits >> 8], axis=0)
        both = both.astype(jnp.float32).astype(jnp.bfloat16)
        byte = lax.dot_general(
            both, spread, (((0,), (0,)), ((), ())), preferred_element_type=jnp.float32
        )
        keep = (byte.astype(jnp.int32) >> bit) & 1
        grad = og[at, :].astype(jnp.float32)
        gp[at, :] = jnp.where(keep == 1, grad, 0.0).astype(jnp.bfloat16)

    lane = iota((half, 128), 1)
    halves = pl.ds(pl.multiple_of(core * half, half), half)

    def send(j, q):
        return pltpu.make_async_remote_copy(
            src_ref=sbuf.at[j], dst_ref=recv.at[me, halves],
            send_sem=ssem, recv_sem=rsem.at[j],
            device_id=(q, core), device_id_type=MESH,
        )

    def forward(p):
        return pltpu.make_async_remote_copy(
            src_ref=recv.at[p, halves], dst_ref=recv.at[p, halves],
            send_sem=fssem, recv_sem=frsem,
            device_id=sib, device_id_type=MESH,
        )

    def keep_own():
        return pltpu.make_async_copy(sbuf.at[peers - 8], recv.at[me, halves], own_sem)

    @pl.loop(0, 8)
    def _(i):
        ahead = group_rows(i, x, y, z, 1)
        for first in range(0, 8, BATCH):
            for u in range(BATCH):
                listed_at = wide[i * 8 + first + u]
                block = listed_at >> 7
                one = jnp.where((listed_at & 127) == lane, 1.0, 0.0)
                for t in range(rows // 128):
                    hot[u * half : (u + 1) * half, t * 128 : (t + 1) * 128] = jnp.where(
                        block == t, one, 0.0
                    ).astype(jnp.bfloat16)
            picked = jnp.dot(hot[...], gp[...], preferred_element_type=jnp.float32)
            for u in range(BATCH):
                sbuf[i * 8 + first + u] = picked[u * half : (u + 1) * half].astype(jnp.bfloat16)

            if first == 0:

                @pl.when(i == 0)
                def _():
                    pl.semaphore_wait(near_sem, len(LINE))

            for u in range(first, first + BATCH):
                if u == 0:

                    @pl.when(i < 7)
                    def _(u=u):
                        send(i * 8 + u, ahead[u]).start()

                    @pl.when(i == 7)
                    def _():
                        keep_own().start()
                else:
                    send(i * 8 + u, ahead[u]).start()

    fill = pltpu.make_async_copy(tv_hbm, tv, tv_sem)
    fill.start()
    for load in loads[5:]:
        load.start()
    loads[3].wait()
    loads[4].wait()
    table_v[...] = layout_tables(
        row_v[...], peer_v[...], row_tiles, peers, table_v.shape[1]
    )
    table_copy = pltpu.make_async_copy(table_v, table_s, table_sem)
    table_copy.start()
    recv[peers] = jnp.zeros(recv.shape[1:], recv.dtype)
    steps[0] = jnp.zeros(steps.shape[1:], steps.dtype)
    loads[5].wait()
    loads[6].wait()
    columns = pl.ds(pl.multiple_of(core * 128, 128), 128)

    @pl.loop(0, row_tiles)
    def _(r):
        at = pl.ds(pl.multiple_of(r * tile, tile), tile)
        nft[r] = nf[at, columns].T

    table_copy.wait()

    @pl.loop(0, 8)
    def _(i):
        for u, p in enumerate(group_rows(i, x, y, z, -1)):
            if u == 0:

                @pl.when(i < 7)
                def _(u=u, p=p):
                    send(i * 8 + u, p).wait_recv()

                @pl.when(i == 7)
                def _():
                    keep_own().wait()
            else:
                send(i * 8 + u, p).wait_recv()
            forward(p).start()

    def wait_bytes(like, send_sem, recv_sem):
        return pltpu.make_async_remote_copy(
            src_ref=like, dst_ref=like, send_sem=send_sem, recv_sem=recv_sem,
            device_id=sib, device_id_type=MESH,
        )

    all_forwards = wait_bytes(sbuf, fssem, frsem)
    all_forwards.wait_recv()

    fill.wait()

    @pl.loop(0, (steps.shape[0] - 1) // UNROLL)
    def _(i):
        for u in range(UNROLL):
            g = i * UNROLL + u
            left = jnp.concatenate([tv[table_s[0, GROUP * g + v]] for v in range(GROUP)], axis=1)
            right = jnp.concatenate([recv[table_s[1, GROUP * g + v]] for v in range(GROUP)], axis=0)
            prod = jnp.dot(left, right, preferred_element_type=jnp.float32)
            steps[g + 1] = jnp.where(table_s[2, g] == 1, steps[g], 0.0) + prod

    def swap(b):
        at = pl.ds(b * GROUP, GROUP)
        return pltpu.make_async_remote_copy(
            src_ref=part.at[at], dst_ref=other.at[at],
            send_sem=pssem.at[b], recv_sem=prsem.at[b],
            device_id=sib, device_id_type=MESH,
        )

    for b in range(row_tiles // GROUP):
        for r in range(b * GROUP, (b + 1) * GROUP):
            part[r] = steps[table_s[3, r]]
        swap(b).start()
    term[...] = jnp.zeros(term.shape, term.dtype)
    for b in range(row_tiles // GROUP):
        swap(b).wait_recv()
        for r in range(b * GROUP, (b + 1) * GROUP):
            agg[r * tile : (r + 1) * tile, :] = (part[r] + other[r]).astype(jnp.bfloat16)
        at = slice(b * GROUP * tile, (b + 1) * GROUP * tile)
        left = jnp.concatenate([nft[b * GROUP + v] for v in range(GROUP)], axis=1)
        term[...] += jnp.dot(left, agg[at, :], preferred_element_type=jnp.float32)

    spot = y * SIDE + z
    piece = red.shape[1]

    def rows_of(s):
        return pl.ds(pl.multiple_of(s * piece, piece), piece)

    mine_at = pl.ds(pl.multiple_of(core * 128 + spot * piece, piece), piece)
    for n, off in enumerate(PLANE):
        q = shifted(off)
        pltpu.make_async_remote_copy(
            src_ref=term.at[rows_of(lax.div(q, SIDE))], dst_ref=red.at[n],
            send_sem=r1s, recv_sem=r1r, device_id=(q, core), device_id_type=MESH,
        ).start()

    @pl.loop(0, rows // 512)
    def _(b):
        at = pl.ds(pl.multiple_of(b * 512, 512), 512)
        ing[at, :] = lax.dot_general(
            agg[at, :], wt[...], (((1,), (1,)), ((), ())), preferred_element_type=jnp.float32
        ).astype(jnp.bfloat16)

    out_copy = pltpu.make_async_copy(ing, ing_hbm, out_sem.at[0])
    out_copy.start()
    mine_sum = term[rows_of(spot), :]
    first = wait_bytes(red, r1s, r1r)
    first.wait_recv()
    for n in range(len(PLANE)):
        mine_sum += red[n]
    line[x] = mine_sum
    for off in LINE:
        pltpu.make_async_remote_copy(
            src_ref=line.at[x], dst_ref=line.at[x],
            send_sem=r2s, recv_sem=r2r, device_id=(shifted(off), core), device_id_type=MESH,
        ).start()
    wait_bytes(sbuf.at[pl.ds(0, peers - 1)], ssem, ssem).wait_send()
    all_forwards.wait_send()
    for b in range(row_tiles // GROUP):
        swap(b).wait_send()
    first.wait_send()
    second = wait_bytes(line.at[pl.ds(0, len(LINE))], r2s, r2r)
    second.wait_recv()
    total = ((line[0] + line[1]) + line[2]) + line[3]
    done[mine_at, :] = total * jnp.float32(scale)
    for off in PLANE:
        pltpu.make_async_remote_copy(
            src_ref=done.at[mine_at], dst_ref=done.at[mine_at],
            send_sem=r3s, recv_sem=r3r, device_id=(shifted(off), core), device_id_type=MESH,
        ).start()
    second.wait_send()
    third = wait_bytes(red, r3s, r3r)
    third.wait_recv()
    mine_half = pl.ds(pl.multiple_of(core * 128, 128), 128)
    fourth = pltpu.make_async_remote_copy(
        src_ref=done.at[mine_half], dst_ref=done.at[mine_half],
        send_sem=r4s, recv_sem=r4r, device_id=sib, device_id_type=MESH,
    )
    fourth.start()
    third.wait_send()
    fourth.wait()
    w_copy = pltpu.make_async_copy(done, wg_hbm, out_sem.at[1])
    w_copy.start()
    out_copy.wait()
    w_copy.wait()


def finish_kernel(ing_in, wg_in, ing_out, wg_out, ing, wg, in_sem, out_sem):
    cuts = [(ing_in, ing, ing_out, pl.ds(n * 512, 512)) for n in range(ing.shape[0] // 512)]
    cuts.append((wg_in, wg, wg_out, pl.ds(0, wg.shape[0])))
    reads = [
        pltpu.make_async_copy(src.at[at], mid.at[at], in_sem.at[n])
        for n, (src, mid, _, at) in enumerate(cuts)
    ]
    writes = [
        pltpu.make_async_copy(mid.at[at], dst.at[at], out_sem.at[n])
        for n, (_, mid, dst, at) in enumerate(cuts)
    ]
    for read in reads:
        read.start()
    for read, write in zip(reads, writes):
        read.wait()
        write.start()
    for write in writes:
        write.wait()


def local(node_feats, out_grad, mask_bits, weight, send_rows, tile_vals, tile_row, tile_peer):
    rows, width = node_feats.shape
    peers, tile = send_rows.shape[1:]
    slots = tile_vals.shape[2]
    half = tile // 2
    row_tiles = rows // tile
    words = mask_bits.shape[1]
    most = -(-(slots + row_tiles * (GROUP - 1)) // GROUP)
    most = -(-most // UNROLL) * UNROLL
    places = -(-most * GROUP // 128) * 128
    piece = width // 2 // 16
    scale = 1.0 / math.sqrt(rows * lax.axis_size("row"))
    anywhere = pl.BlockSpec(memory_space=pl.ANY)
    bf16, f32, i32 = jnp.bfloat16, jnp.float32, jnp.int32
    dma = pltpu.SemaphoreType.DMA
    parts_shape = (
        jax.ShapeDtypeStruct((rows, width), bf16),
        jax.ShapeDtypeStruct((width, width), f32),
    )
    parts = pl.pallas_call(
        lambda *refs: kernel(scale, *refs),
        out_shape=parts_shape,
        in_specs=[anywhere] * 8,
        out_specs=(anywhere, anywhere),
        scratch_shapes=[
            pltpu.VMEM((rows, width), bf16),
            pltpu.VMEM((words, rows), i32),
            pltpu.VMEM((peers, tile), i32),
            pltpu.VMEM((1, slots), i32),
            pltpu.VMEM((1, slots), i32),
            pltpu.VMEM((rows, width), bf16),
            pltpu.VMEM((width, width), bf16),
            pltpu.VMEM((slots, tile, tile), bf16),
            pltpu.VMEM((rows, width), bf16),
            pltpu.VMEM((128, 128), i32),
            pltpu.VMEM((128, 128), i32),
            pltpu.VMEM((peers, half, 128), i32),
            pltpu.VMEM((BATCH * half, rows), bf16),
            pltpu.VMEM((peers, half, width), bf16),
            pltpu.VMEM((peers + 1, tile, width), bf16),
            pltpu.VMEM((8, places), i32),
            pltpu.SMEM((8, places), i32),
            pltpu.VMEM((most + 1, tile, width), f32),
            pltpu.VMEM((row_tiles, tile, width), f32),
            pltpu.VMEM((row_tiles, tile, width), f32),
            pltpu.VMEM((row_tiles, width // 2, tile), bf16),
            pltpu.VMEM((rows, width), bf16),
            pltpu.VMEM((rows, width), bf16),
            pltpu.VMEM((width // 2, width), f32),
            pltpu.VMEM((len(PLANE), piece, width), f32),
            pltpu.VMEM((SIDE, piece, width), f32),
            pltpu.VMEM((width, width), f32),
            dma((7,)), dma, dma, dma, dma((2,)),
            pltpu.SemaphoreType.REGULAR, dma, dma((peers,)), dma, dma,
            dma((row_tiles // GROUP,)), dma((row_tiles // GROUP,)),
            dma, dma, dma, dma, dma, dma, dma, dma,
        ],
        compiler_params=pltpu.CompilerParams(
            collective_id=0, has_side_effects=True, vmem_limit_bytes=60 * 2**20
        ),
        name="layer",
    )(
        out_grad, mask_bits.T, send_rows[0], tile_row[0], tile_peer[0],
        node_feats, weight, tile_vals[0, 0],
    )
    return pl.pallas_call(
        finish_kernel,
        out_shape=parts_shape,
        in_specs=[anywhere] * 2,
        out_specs=(anywhere, anywhere),
        scratch_shapes=[
            pltpu.VMEM((rows, width), bf16),
            pltpu.VMEM((width, width), f32),
            dma((rows // 512 + 1,)),
            dma((rows // 512 + 1,)),
        ],
        name="finish",
    )(*parts)


def solution(mesh):
    placed = (
        P("row", None),
        P("row", None),
        P("row", None),
        P(),
        P("row", None, None),
        P("row", "rep", None, None, None),
        P("row", "rep", None),
        P("row", "rep", None),
    )
    return jax.shard_map(
        local, mesh=mesh, in_specs=placed, out_specs=(P("row", None), P()), check_vma=False
    )
```

```python
import math

import jax
import jax.numpy as jnp
from jax import lax
from jax.experimental import pallas as pl
from jax.experimental.pallas import tpu as pltpu
from jax.sharding import PartitionSpec as P

MESH = pl.DeviceIdType.MESH
SIDE = 4
UORDER = (0, 7, 1, 6, 2, 5, 3, 4)
GROUP = 4
UNROLL = 20
BATCH = 4
PLANE = [(0, a, b) for a in range(4) for b in range(4) if (a, b) != (0, 0)]
LINE = [(a, 0, 0) for a in range(1, 4)]


def ring(v):
    return [v] + [lax.rem(v + d, SIDE) for d in range(1, SIDE)]


def group_rows(i, x, y, z):
    g = 7 - i
    odd = (lax.rem(g, 2), lax.rem(lax.div(g, 2), 2), lax.div(g, 4))
    at = [
        [lax.rem(v + o, SIDE), lax.rem(v + o + 2, SIDE)]
        for v, o in zip((x, y, z), odd)
    ]
    return [
        at[1][(w >> 1) & 1] * (SIDE * SIDE) + at[2][w >> 2] * SIDE + at[0][w & 1] for w in UORDER
    ]


def iota(shape, dim):
    return lax.broadcasted_iota(jnp.int32, shape, dim)


def place_of(peer, x, y, z):
    dx, dy, dz = (x + 4 - (peer & 3)) & 3, (y + 4 - (peer >> 4)) & 3, (z + 4 - ((peer >> 2) & 3)) & 3
    g = (dx & 1) + 2 * (dy & 1) + 4 * (dz & 1)
    w = (dx >> 1) + 2 * (dy >> 1) + 4 * (dz >> 1)
    return 8 * (7 - g) + jnp.where(w < 4, 2 * w, 15 - 2 * w)


def layout_tables(row, peer, row_tiles, zero_peer, places):
    slots = row.shape[1]
    key = jnp.where(row < 0, row_tiles, row)
    key_down = jnp.broadcast_to(key, (128, slots)).T
    peer_down = jnp.broadcast_to(peer, (128, slots)).T
    down = iota((slots, 128), 0)
    across = iota((slots, 128), 1)
    count = jnp.sum((key_down == across).astype(jnp.int32), axis=0, keepdims=True)
    groups = jnp.where(iota((1, 128), 1) < row_tiles, (count + GROUP - 1) // GROUP, 0)
    groups_down = jnp.broadcast_to(groups, (128, 128)).T
    r_down, r_across = iota((128, 128), 0), iota((128, 128), 1)
    first = jnp.sum(jnp.where(r_down < r_across, groups_down, 0), axis=0, keepdims=True)
    first_down = jnp.broadcast_to(first, (128, 128)).T

    spots = []
    for b in range(slots // 128):
        key_here = key[:, b * 128 : (b + 1) * 128]
        before = (key_down == key_here) & (down < across + b * 128)
        rank = jnp.sum(before.astype(jnp.int32), axis=0, keepdims=True)
        base = jnp.sum(jnp.where(r_down < key_here, groups_down, 0), axis=0, keepdims=True)
        spots.append(jnp.where(key_here < row_tiles, base * GROUP + rank, -1))
    spot_down = jnp.broadcast_to(jnp.concatenate(spots, axis=1), (128, slots)).T

    slot_at, peer_at, goes_on = [], [], []
    for b in range(places // 128):
        hit = spot_down == across + b * 128
        slot_at.append(jnp.sum(jnp.where(hit, down, 0), axis=0, keepdims=True))
        peer_at.append(
            jnp.sum(jnp.where(hit, peer_down - zero_peer, 0), axis=0, keepdims=True) + zero_peer
        )
        opens = (first_down == r_across + b * 128) & (groups_down > 0)
        goes_on.append(1 - jnp.sum(opens.astype(jnp.int32), axis=0, keepdims=True))
    last = jnp.where(groups > 0, first + groups, 0)
    last = jnp.concatenate([last, jnp.zeros((1, places - 128), jnp.int32)], axis=1)
    rows = [jnp.concatenate(part, axis=1) for part in (slot_at, peer_at, goes_on)] + [last]
    return jnp.concatenate(rows + [jnp.zeros((8 - len(rows), places), jnp.int32)], axis=0)


def kernel(
    scale,
    og_hbm, mb_hbm, sr_hbm, row_hbm, peer_hbm, nf_hbm, wt_hbm, tv_hbm,
    ing_hbm, wg_hbm,
    og, mb, sr, row_v, peer_v, nf, wt, tv,
    gp, listed, turned, wide, hot, sbuf, recv, table_v, table_s,
    steps, part, other, nft, ing, agg, term, red, line, done,
    in_sem, tv_sem, table_sem, own_sem, out_sem,
    near_sem, ssem, rsem, fssem, frsem, pssem, prsem, r1s, r1r, r2s, r2r, r3s, r3r, r4s, r4r, r5s, r5r,
):
    me = lax.axis_index("row")
    core = lax.axis_index("rep")
    x, z, y = lax.rem(me, SIDE), lax.rem(lax.div(me, SIDE), SIDE), lax.div(me, SIDE * SIDE)
    xs, ys, zs = ring(x), ring(y), ring(z)

    def shifted(off):
        return ys[off[1]] * (SIDE * SIDE) + zs[off[2]] * SIDE + xs[off[0]]

    rows, width = gp.shape
    peers, half = sbuf.shape[:2]
    tile = 2 * half
    row_tiles = rows // tile
    sib = (me, 1 - core)

    loads = [
        pltpu.make_async_copy(src, dst, in_sem.at[n])
        for n, (src, dst) in enumerate(
            (
                (sr_hbm, sr), (mb_hbm, mb), (og_hbm, og), (row_hbm, row_v),
                (peer_hbm, peer_v), (nf_hbm, nf), (wt_hbm, wt),
            )
        )
    ]
    for load in loads[:5]:
        load.start()

    barrier = pltpu.get_barrier_semaphore()
    pl.semaphore_signal(barrier, inc=1, device_id=sib, device_id_type=MESH)
    for off in LINE + PLANE:
        pl.semaphore_signal(
            barrier, inc=1, device_id=(shifted(off), core), device_id_type=MESH
        )
    greeted = 1 + len(LINE) + len(PLANE)

    loads[0].wait()
    listed[...] = jnp.full(listed.shape, -1, jnp.int32)

    @pl.loop(0, 8)
    def _(i):
        for u, q in enumerate(group_rows(i, x, y, z)):
            listed[pl.ds(i * 8 + u, 1), :] = sr[pl.ds(q, 1), :]

    turned[...] = listed[...].T
    mine = turned[pl.ds(pl.multiple_of(core * half, half), half), :]
    for j in range(64):
        wide[j] = jnp.broadcast_to(mine[:, j : j + 1], (half, 128))

    pl.semaphore_wait(barrier, greeted)
    for off in LINE:
        pl.semaphore_signal(
            near_sem, inc=1, device_id=(shifted(off), core), device_id_type=MESH
        )

    words = mb.shape[0]
    feature = iota((2 * words, width), 1)
    byte_at = iota((2 * words, width), 0)
    spread = (feature // 16 == byte_at % words) & ((feature % 16 >= 8) == (byte_at >= words))
    spread = jnp.where(spread, 1.0, 0.0).astype(jnp.bfloat16)
    step = 256
    bit = iota((step, width), 1) % 8
    loads[1].wait()
    loads[2].wait()

    @pl.loop(0, rows // step)
    def _(b):
        at = pl.ds(pl.multiple_of(b * step, step), step)
        bits = mb[:, at]
        both = jnp.concatenate([bits & 255, bits >> 8], axis=0)
        both = both.astype(jnp.float32).astype(jnp.bfloat16)
        byte = lax.dot_general(
            both, spread, (((0,), (0,)), ((), ())), preferred_element_type=jnp.float32
        )
        keep = (byte.astype(jnp.int32) >> bit) & 1
        grad = og[at, :].astype(jnp.float32)
        gp[at, :] = jnp.where(keep == 1, grad, 0.0).astype(jnp.bfloat16)

    lane = iota((half, 128), 1)
    halves = pl.ds(pl.multiple_of(core * half, half), half)

    def send(j, q):
        return pltpu.make_async_remote_copy(
            src_ref=sbuf.at[j], dst_ref=recv.at[j, halves],
            send_sem=ssem, recv_sem=rsem.at[lax.div(j, 8)],
            device_id=(q, core), device_id_type=MESH,
        )

    def wait_bytes(like, send_sem, recv_sem):
        return pltpu.make_async_remote_copy(
            src_ref=like, dst_ref=like, send_sem=send_sem, recv_sem=recv_sem,
            device_id=sib, device_id_type=MESH,
        )

    def keep_own():
        return pltpu.make_async_copy(sbuf.at[peers - 8], recv.at[peers - 8, halves], own_sem)

    @pl.loop(0, 8)
    def _(i):
        ahead = group_rows(i, x, y, z)
        for first in range(0, 8, BATCH):
            for u in range(BATCH):
                listed_at = wide[i * 8 + first + u]
                block = listed_at >> 7
                one = jnp.where((listed_at & 127) == lane, 1.0, 0.0)
                for t in range(rows // 128):
                    hot[u * half : (u + 1) * half, t * 128 : (t + 1) * 128] = jnp.where(
                        block == t, one, 0.0
                    ).astype(jnp.bfloat16)
            picked = jnp.dot(hot[...], gp[...], preferred_element_type=jnp.float32)
            for u in range(BATCH):
                sbuf[i * 8 + first + u] = picked[u * half : (u + 1) * half].astype(jnp.bfloat16)

            if first == 0:

                @pl.when(i == 0)
                def _():
                    pl.semaphore_wait(near_sem, len(LINE))

            for u in range(first, first + BATCH):
                if u == 0:

                    @pl.when(i < 7)
                    def _(u=u):
                        send(i * 8 + u, ahead[u]).start()

                    @pl.when(i == 7)
                    def _():
                        keep_own().start()
                else:
                    send(i * 8 + u, ahead[u]).start()

    fill = pltpu.make_async_copy(tv_hbm, tv, tv_sem)
    fill.start()
    for load in loads[5:]:
        load.start()
    loads[3].wait()
    loads[4].wait()
    table_v[...] = layout_tables(
        row_v[...], place_of(peer_v[...], x, y, z), row_tiles, peers, table_v.shape[1]
    )
    table_copy = pltpu.make_async_copy(table_v, table_s, table_sem)
    table_copy.start()
    recv[peers] = jnp.zeros(recv.shape[1:], recv.dtype)
    steps[0] = jnp.zeros(steps.shape[1:], steps.dtype)
    loads[5].wait()
    loads[6].wait()

    @pl.loop(0, row_tiles)
    def _(r):
        at = pl.ds(pl.multiple_of(r * tile, tile), tile)
        nft[r] = nf[at, :].T

    table_copy.wait()

    for i in range(8):
        if i < 7:
            wait_bytes(sbuf.at[pl.ds(0, 8)], ssem, rsem.at[i]).wait_recv()
        else:
            wait_bytes(sbuf.at[pl.ds(0, 7)], ssem, rsem.at[i]).wait_recv()
            keep_own().wait()
        here = recv.at[pl.ds(i * 8, 8), halves]
        pltpu.make_async_remote_copy(
            src_ref=here, dst_ref=here, send_sem=fssem, recv_sem=frsem,
            device_id=sib, device_id_type=MESH,
        ).start()
    all_forwards = wait_bytes(sbuf, fssem, frsem)
    all_forwards.wait_recv()

    fill.wait()

    @pl.loop(0, (steps.shape[0] - 1) // UNROLL)
    def _(i):
        for u in range(UNROLL):
            g = i * UNROLL + u
            left = jnp.concatenate([tv[table_s[0, GROUP * g + v]] for v in range(GROUP)], axis=1)
            right = jnp.concatenate([recv[table_s[1, GROUP * g + v]] for v in range(GROUP)], axis=0)
            prod = jnp.dot(left, right, preferred_element_type=jnp.float32)
            steps[g + 1] = jnp.where(table_s[2, g] == 1, steps[g], 0.0) + prod

    lanes = width // 2
    mine_cols = pl.ds(pl.multiple_of(core * lanes, lanes), lanes)
    sib_cols = pl.ds(pl.multiple_of((1 - core) * lanes, lanes), lanes)

    def swap(b):
        at = pl.ds(b * GROUP, GROUP)
        return pltpu.make_async_remote_copy(
            src_ref=part.at[at], dst_ref=other.at[at],
            send_sem=pssem.at[b], recv_sem=prsem.at[b],
            device_id=sib, device_id_type=MESH,
        )

    for b in range(row_tiles // GROUP):
        for r in range(b * GROUP, (b + 1) * GROUP):
            part[r] = steps[table_s[3, r], :, sib_cols]
        swap(b).start()
    term[...] = jnp.zeros(term.shape, term.dtype)
    for b in range(row_tiles // GROUP):
        swap(b).wait_recv()
        for r in range(b * GROUP, (b + 1) * GROUP):
            mine_sum = steps[table_s[3, r], :, mine_cols] + other[r]
            agg[core, r * tile : (r + 1) * tile, :] = mine_sum.astype(jnp.bfloat16)
        left = jnp.concatenate([nft[b * GROUP + v] for v in range(GROUP)], axis=1)
        right = agg[core, b * GROUP * tile : (b + 1) * GROUP * tile, :]
        term[...] += jnp.dot(left, right, preferred_element_type=jnp.float32)

    odds = [lax.rem(v, 2) for v in (x, y, z)]
    ends = [lax.rem(lax.div(v + 1, 2), 2) for v in (x, y, z)]
    piece = red.shape[1]

    def rows_of(s):
        return pl.ds(pl.multiple_of(s * piece, piece), piece)

    def in_cube(n):
        bits = (n & 1, (n >> 1) & 1, n >> 2)
        px, py, pz = [v + b * (1 - 2 * o) for v, o, b in zip((x, y, z), odds, bits)]
        ox, oy, oz = [o + b * (1 - 2 * o) for o, b in zip(ends, bits)]
        return py * (SIDE * SIDE) + pz * SIDE + px, ox + 2 * oy + 4 * oz

    def facing(n):
        bits = (n & 1, (n >> 1) & 1, n >> 2)
        px, py, pz = [3 - v if b else v for v, b in zip((x, y, z), bits)]
        return py * (SIDE * SIDE) + pz * SIDE + px

    spot = in_cube(0)[1]
    cube = lax.div(x, 2) + 2 * lax.div(y, 2) + 4 * lax.div(z, 2)
    for n in range(1, 8):
        q, to = in_cube(n)
        pltpu.make_async_remote_copy(
            src_ref=term.at[rows_of(to)], dst_ref=red.at[n - 1],
            send_sem=r1s, recv_sem=r1r, device_id=(q, core), device_id_type=MESH,
        ).start()
    give = pltpu.make_async_remote_copy(
        src_ref=agg.at[core], dst_ref=agg.at[core],
        send_sem=r5s, recv_sem=r5r, device_id=sib, device_id_type=MESH,
    )
    give.start()
    mine_sum = term[rows_of(spot), :]
    first = wait_bytes(red, r1s, r1r)
    first.wait_recv()
    for n in range(7):
        mine_sum += red[n]
    line[cube] = mine_sum
    for n in range(1, 8):
        pltpu.make_async_remote_copy(
            src_ref=line.at[cube], dst_ref=line.at[cube],
            send_sem=r2s, recv_sem=r2r, device_id=(facing(n), core), device_id_type=MESH,
        ).start()

    give.wait_recv()

    @pl.loop(0, rows // 512)
    def _(b):
        at = pl.ds(pl.multiple_of(b * 512, 512), 512)
        total = sum(
            lax.dot_general(
                agg[h, at, :], wt[:, h * lanes : (h + 1) * lanes], (((1,), (1,)), ((), ())),
                preferred_element_type=jnp.float32,
            )
            for h in range(2)
        )
        ing[at, :] = total.astype(jnp.bfloat16)

    out_copy = pltpu.make_async_copy(ing, ing_hbm, out_sem.at[0])
    out_copy.start()
    second = wait_bytes(line.at[pl.ds(0, 7)], r2s, r2r)
    second.wait_recv()
    total = line[0]
    for n in range(1, 8):
        total += line[n]
    done[core, rows_of(spot), :] = total * jnp.float32(scale)
    for n in range(1, 8):
        pltpu.make_async_remote_copy(
            src_ref=done.at[core, rows_of(spot)], dst_ref=done.at[core, rows_of(spot)],
            send_sem=r3s, recv_sem=r3r, device_id=(in_cube(n)[0], core), device_id_type=MESH,
        ).start()
    wait_bytes(sbuf.at[pl.ds(0, peers - 1)], ssem, ssem).wait_send()
    all_forwards.wait_send()
    for b in range(row_tiles // GROUP):
        swap(b).wait_send()
    first.wait_send()
    second.wait_send()
    give.wait_send()
    third = wait_bytes(red, r3s, r3r)
    third.wait_recv()
    fourth = pltpu.make_async_remote_copy(
        src_ref=done.at[core], dst_ref=done.at[core],
        send_sem=r4s, recv_sem=r4r, device_id=sib, device_id_type=MESH,
    )
    fourth.start()
    mine_copy = pltpu.make_async_copy(done.at[core], wg_hbm.at[core], out_sem.at[1])
    mine_copy.start()
    third.wait_send()
    fourth.wait()
    sib_copy = pltpu.make_async_copy(done.at[1 - core], wg_hbm.at[1 - core], out_sem.at[2])
    sib_copy.start()
    out_copy.wait()
    mine_copy.wait()
    sib_copy.wait()


def finish_kernel(ing_in, wg_in, ing_out, wg_out, ing, wg, in_sem, out_sem):
    cuts = [
        (ing_in.at[at], ing.at[at], ing_out.at[at])
        for at in (pl.ds(n * 512, 512) for n in range(ing.shape[0] // 512))
    ]
    lanes = wg.shape[2]
    cuts += [
        (wg_in.at[h], wg.at[h], wg_out.at[:, pl.ds(h * lanes, lanes)]) for h in range(2)
    ]
    reads = [
        pltpu.make_async_copy(src, mid, in_sem.at[n])
        for n, (src, mid, _) in enumerate(cuts)
    ]
    writes = [
        pltpu.make_async_copy(mid, dst, out_sem.at[n])
        for n, (_, mid, dst) in enumerate(cuts)
    ]
    for read in reads:
        read.start()
    for read, write in zip(reads, writes):
        read.wait()
        write.start()
    for write in writes:
        write.wait()


def local(node_feats, out_grad, mask_bits, weight, send_rows, tile_vals, tile_row, tile_peer):
    rows, width = node_feats.shape
    peers, tile = send_rows.shape[1:]
    slots = tile_vals.shape[2]
    half = tile // 2
    row_tiles = rows // tile
    words = mask_bits.shape[1]
    most = -(-(slots + row_tiles * (GROUP - 1)) // GROUP)
    most = -(-most // UNROLL) * UNROLL
    places = -(-most * GROUP // 128) * 128
    piece = width // 8
    lanes = width // 2
    scale = 1.0 / math.sqrt(rows * lax.axis_size("row"))
    anywhere = pl.BlockSpec(memory_space=pl.ANY)
    bf16, f32, i32 = jnp.bfloat16, jnp.float32, jnp.int32
    dma = pltpu.SemaphoreType.DMA
    in_shape = jax.ShapeDtypeStruct((rows, width), bf16)
    parts = pl.pallas_call(
        lambda *refs: kernel(scale, *refs),
        out_shape=(in_shape, jax.ShapeDtypeStruct((2, width, lanes), f32)),
        in_specs=[anywhere] * 8,
        out_specs=(anywhere, anywhere),
        scratch_shapes=[
            pltpu.VMEM((rows, width), bf16),
            pltpu.VMEM((words, rows), i32),
            pltpu.VMEM((peers, tile), i32),
            pltpu.VMEM((1, slots), i32),
            pltpu.VMEM((1, slots), i32),
            pltpu.VMEM((rows, width), bf16),
            pltpu.VMEM((width, width), bf16),
            pltpu.VMEM((slots, tile, tile), bf16),
            pltpu.VMEM((rows, width), bf16),
            pltpu.VMEM((128, 128), i32),
            pltpu.VMEM((128, 128), i32),
            pltpu.VMEM((peers, half, 128), i32),
            pltpu.VMEM((BATCH * half, rows), bf16),
            pltpu.VMEM((peers, half, width), bf16),
            pltpu.VMEM((peers + 1, tile, width), bf16),
            pltpu.VMEM((8, places), i32),
            pltpu.SMEM((8, places), i32),
            pltpu.VMEM((most + 1, tile, width), f32),
            pltpu.VMEM((row_tiles, tile, lanes), f32),
            pltpu.VMEM((row_tiles, tile, lanes), f32),
            pltpu.VMEM((row_tiles, width, tile), bf16),
            pltpu.VMEM((rows, width), bf16),
            pltpu.VMEM((2, rows, lanes), bf16),
            pltpu.VMEM((width, lanes), f32),
            pltpu.VMEM((7, piece, lanes), f32),
            pltpu.VMEM((8, piece, lanes), f32),
            pltpu.VMEM((2, width, lanes), f32),
            dma((7,)), dma, dma, dma, dma((3,)),
            pltpu.SemaphoreType.REGULAR, dma, dma((8,)), dma, dma,
            dma((row_tiles // GROUP,)), dma((row_tiles // GROUP,)),
            dma, dma, dma, dma, dma, dma, dma, dma, dma, dma,
        ],
        compiler_params=pltpu.CompilerParams(
            collective_id=0, has_side_effects=True, vmem_limit_bytes=60 * 2**20
        ),
        name="layer",
    )(
        out_grad, mask_bits.T, send_rows[0], tile_row[0], tile_peer[0],
        node_feats, weight, tile_vals[0, 0],
    )
    return pl.pallas_call(
        finish_kernel,
        out_shape=(in_shape, jax.ShapeDtypeStruct((width, width), f32)),
        in_specs=[anywhere] * 2,
        out_specs=(anywhere, anywhere),
        scratch_shapes=[
            pltpu.VMEM((rows, width), bf16),
            pltpu.VMEM((2, width, lanes), f32),
            dma((rows // 512 + 2,)),
            dma((rows // 512 + 2,)),
        ],
        name="finish",
    )(*parts)


def solution(mesh):
    placed = (
        P("row", None),
        P("row", None),
        P("row", None),
        P(),
        P("row", None, None),
        P("row", "rep", None, None, None),
        P("row", "rep", None),
        P("row", "rep", None),
    )
    return jax.shard_map(
        local, mesh=mesh, in_specs=placed, out_specs=(P("row", None), P()), check_vma=False
    )
```

```python
import math

import jax
import jax.numpy as jnp
from jax import lax
from jax.experimental import pallas as pl
from jax.experimental.pallas import tpu as pltpu
from jax.sharding import PartitionSpec as P

MESH = pl.DeviceIdType.MESH
SIDE = 4
UORDER = (0, 7, 1, 6, 2, 5, 3, 4)
GROUP = 8
CHUNK = 4
UNROLL = 40
PLANE = [(0, a, b) for a in range(4) for b in range(4) if (a, b) != (0, 0)]
LINE = [(a, 0, 0) for a in range(1, 4)]


def ring(v):
    return [v] + [lax.rem(v + d, SIDE) for d in range(1, SIDE)]


def group_rows(i, x, y, z):
    g = 7 - i
    odd = (lax.rem(g, 2), lax.rem(lax.div(g, 2), 2), lax.div(g, 4))
    at = [
        [lax.rem(v + o, SIDE), lax.rem(v + o + 2, SIDE)]
        for v, o in zip((x, y, z), odd)
    ]
    return [
        at[1][(w >> 1) & 1] * (SIDE * SIDE) + at[2][w >> 2] * SIDE + at[0][w & 1] for w in UORDER
    ]


def iota(shape, dim):
    return lax.broadcasted_iota(jnp.int32, shape, dim)


def place_of(peer, x, y, z):
    dx, dy, dz = (x + 4 - (peer & 3)) & 3, (y + 4 - (peer >> 4)) & 3, (z + 4 - ((peer >> 2) & 3)) & 3
    g = (dx & 1) + 2 * (dy & 1) + 4 * (dz & 1)
    w = (dx >> 1) + 2 * (dy >> 1) + 4 * (dz >> 1)
    return 8 * (7 - g) + jnp.where(w < 4, 2 * w, 15 - 2 * w)


def layout_tables(row, peer, row_tiles, zero_peer, places):
    slots = row.shape[1]
    key = jnp.where(row < 0, row_tiles, row)
    key_down = jnp.broadcast_to(key, (128, slots)).T
    peer_down = jnp.broadcast_to(peer, (128, slots)).T
    down = iota((slots, 128), 0)
    across = iota((slots, 128), 1)
    count = jnp.sum((key_down == across).astype(jnp.int32), axis=0, keepdims=True)
    groups = jnp.where(iota((1, 128), 1) < row_tiles, (count + GROUP - 1) // GROUP, 0)
    groups_down = jnp.broadcast_to(groups, (128, 128)).T
    r_down, r_across = iota((128, 128), 0), iota((128, 128), 1)
    first = jnp.sum(jnp.where(r_down < r_across, groups_down, 0), axis=0, keepdims=True)
    first_down = jnp.broadcast_to(first, (128, 128)).T

    spots = []
    for b in range(slots // 128):
        key_here = key[:, b * 128 : (b + 1) * 128]
        before = (key_down == key_here) & (down < across + b * 128)
        rank = jnp.sum(before.astype(jnp.int32), axis=0, keepdims=True)
        base = jnp.sum(jnp.where(r_down < key_here, groups_down, 0), axis=0, keepdims=True)
        spots.append(jnp.where(key_here < row_tiles, base * GROUP + rank, -1))
    spot_down = jnp.broadcast_to(jnp.concatenate(spots, axis=1), (128, slots)).T

    slot_at, peer_at, goes_on = [], [], []
    for b in range(places // 128):
        hit = spot_down == across + b * 128
        slot_at.append(jnp.sum(jnp.where(hit, down, 0), axis=0, keepdims=True))
        peer_at.append(
            jnp.sum(jnp.where(hit, peer_down - zero_peer, 0), axis=0, keepdims=True) + zero_peer
        )
        opens = (first_down == r_across + b * 128) & (groups_down > 0)
        goes_on.append(1 - jnp.sum(opens.astype(jnp.int32), axis=0, keepdims=True))
    last = jnp.where(groups > 0, first + groups, 0)
    last = jnp.concatenate([last, jnp.zeros((1, places - 128), jnp.int32)], axis=1)
    rows = [jnp.concatenate(part, axis=1) for part in (slot_at, peer_at, goes_on)] + [last]
    return jnp.concatenate(rows + [jnp.zeros((8 - len(rows), places), jnp.int32)], axis=0)


def kernel(
    scale,
    og_hbm, mb_hbm, sr_hbm, row_hbm, peer_hbm, nf_hbm, wt_hbm, tv_hbm,
    ing_hbm, wg_hbm,
    og, mb, sr, row_v, peer_v, nf, wt, tv,
    gp, listed, turned, wide, hot, sbuf, recv_a, recv_b, table_v, table_s,
    later, steps, sums, part, other, nft, ing, agg, term, red, line, done,
    in_sem, tv_sem, table_sem, own_sem, out_sem,
    near_sem, ssem, rsem, fssem, frsem, pssem, prsem, r1s, r1r, r2s, r2r, r3s, r3r, r4s, r4r, r5s, r5r,
):
    me = lax.axis_index("row")
    core = lax.axis_index("rep")
    x, z, y = lax.rem(me, SIDE), lax.rem(lax.div(me, SIDE), SIDE), lax.div(me, SIDE * SIDE)
    xs, ys, zs = ring(x), ring(y), ring(z)

    def shifted(off):
        return ys[off[1]] * (SIDE * SIDE) + zs[off[2]] * SIDE + xs[off[0]]

    rows, width = gp.shape
    peers, quarter = sbuf.shape[1:3]
    half = 2 * quarter
    tile = 2 * half
    recv = (recv_a, recv_b)
    row_tiles = rows // tile
    sib = (me, 1 - core)

    loads = [
        pltpu.make_async_copy(src, dst, in_sem.at[n])
        for n, (src, dst) in enumerate(
            (
                (sr_hbm, sr), (mb_hbm, mb), (og_hbm, og), (row_hbm, row_v),
                (peer_hbm, peer_v), (nf_hbm, nf), (wt_hbm, wt),
            )
        )
    ]
    for load in loads[:5]:
        load.start()

    barrier = pltpu.get_barrier_semaphore()
    pl.semaphore_signal(barrier, inc=1, device_id=sib, device_id_type=MESH)
    for off in LINE + PLANE:
        pl.semaphore_signal(
            barrier, inc=1, device_id=(shifted(off), core), device_id_type=MESH
        )
    greeted = 1 + len(LINE) + len(PLANE)

    loads[0].wait()
    listed[...] = jnp.full(listed.shape, -1, jnp.int32)

    @pl.loop(0, 8)
    def _(i):
        for u, q in enumerate(group_rows(i, x, y, z)):
            listed[pl.ds(i * 8 + u, 1), :] = sr[pl.ds(q, 1), :]

    turned[...] = listed[...].T
    mine = jnp.concatenate(
        [
            turned[pl.ds(pl.multiple_of(ph * half + core * quarter, quarter), quarter), :]
            for ph in range(2)
        ],
        axis=0,
    )
    for j in range(64):
        wide[j] = jnp.broadcast_to(mine[:, j : j + 1], (half, 128))

    pl.semaphore_wait(barrier, greeted)
    for off in LINE:
        pl.semaphore_signal(
            near_sem, inc=1, device_id=(shifted(off), core), device_id_type=MESH
        )

    words = mb.shape[0]
    feature = iota((2 * words, width), 1)
    byte_at = iota((2 * words, width), 0)
    spread = (feature // 16 == byte_at % words) & ((feature % 16 >= 8) == (byte_at >= words))
    spread = jnp.where(spread, 1.0, 0.0).astype(jnp.bfloat16)
    step = 256
    bit = iota((step, width), 1) % 8
    loads[1].wait()
    loads[2].wait()

    @pl.loop(0, rows // step)
    def _(b):
        at = pl.ds(pl.multiple_of(b * step, step), step)
        bits = mb[:, at]
        both = jnp.concatenate([bits & 255, bits >> 8], axis=0)
        both = both.astype(jnp.float32).astype(jnp.bfloat16)
        byte = lax.dot_general(
            both, spread, (((0,), (0,)), ((), ())), preferred_element_type=jnp.float32
        )
        keep = (byte.astype(jnp.int32) >> bit) & 1
        grad = og[at, :].astype(jnp.float32)
        gp[at, :] = jnp.where(keep == 1, grad, 0.0).astype(jnp.bfloat16)

    lane = iota((quarter, 128), 1)
    mine_rows = pl.ds(pl.multiple_of(core * quarter, quarter), quarter)

    def send(ph, t, u, q):
        return pltpu.make_async_remote_copy(
            src_ref=sbuf.at[ph, (t - 8 * ph) * 8 + u],
            dst_ref=recv[ph].at[(t - 8 * ph) * 8 + u, mine_rows],
            send_sem=ssem, recv_sem=rsem.at[t],
            device_id=(q, core), device_id_type=MESH,
        )

    def wait_bytes(like, send_sem, recv_sem):
        return pltpu.make_async_remote_copy(
            src_ref=like, dst_ref=like, send_sem=send_sem, recv_sem=recv_sem,
            device_id=sib, device_id_type=MESH,
        )

    def keep_own(ph):
        return pltpu.make_async_copy(
            sbuf.at[ph, peers - 8], recv[ph].at[peers - 8, mine_rows], own_sem.at[ph]
        )

    for ph in range(2):

        @pl.loop(8 * ph, 8 * ph + 8)
        def _(t, ph=ph):
            i = t - 8 * ph
            ahead = group_rows(i, x, y, z)
            for u in range(8):
                listed_at = wide[i * 8 + u, ph * quarter : (ph + 1) * quarter]
                block = listed_at >> 7
                one = jnp.where((listed_at & 127) == lane, 1.0, 0.0)
                for c in range(rows // 128):
                    hot[u * quarter : (u + 1) * quarter, c * 128 : (c + 1) * 128] = jnp.where(
                        block == c, one, 0.0
                    ).astype(jnp.bfloat16)
            picked = jnp.dot(hot[...], gp[...], preferred_element_type=jnp.float32)
            for u in range(8):
                sbuf[ph, i * 8 + u] = picked[u * quarter : (u + 1) * quarter].astype(jnp.bfloat16)

            @pl.when(t == 0)
            def _():
                pl.semaphore_wait(near_sem, len(LINE))

            @pl.when(i < 7)
            def _():
                send(ph, t, 0, ahead[0]).start()

            @pl.when(i == 7)
            def _():
                keep_own(ph).start()

            for u in range(1, 8):
                send(ph, t, u, ahead[u]).start()

    fill = pltpu.make_async_copy(tv_hbm, tv, tv_sem)
    fill.start()
    for load in loads[5:]:
        load.start()
    loads[3].wait()
    loads[4].wait()
    table_v[...] = layout_tables(
        row_v[...], place_of(peer_v[...], x, y, z), row_tiles, peers, table_v.shape[1]
    )
    table_copy = pltpu.make_async_copy(table_v, table_s, table_sem)
    table_copy.start()
    for buf in recv:
        buf[peers] = jnp.zeros(buf.shape[1:], buf.dtype)
    steps[0] = jnp.zeros(steps.shape[1:], steps.dtype)
    loads[5].wait()
    loads[6].wait()

    @pl.loop(0, row_tiles)
    def _(r):
        at = pl.ds(pl.multiple_of(r * tile, tile), tile)
        nft[r] = nf[at, :].T

    table_copy.wait()

    def take(ph, groups):
        for i in groups:
            lists = 8 if i < 7 else 7
            wait_bytes(sbuf.at[0, pl.ds(0, lists)], ssem, rsem.at[8 * ph + i]).wait_recv()
            if i == 7:
                keep_own(ph).wait()
            here = recv[ph].at[pl.ds(i * 8, 8), mine_rows]
            pltpu.make_async_remote_copy(
                src_ref=here, dst_ref=here, send_sem=fssem.at[ph], recv_sem=frsem.at[ph],
                device_id=sib, device_id_type=MESH,
            ).start()

    def taken(ph):
        wait_bytes(sbuf.at[0], fssem.at[ph], frsem.at[ph]).wait_recv()

    def products(ph, start, stop):
        @pl.loop(start, stop)
        def _(i):
            for n in range(UNROLL):
                g = i * UNROLL + n
                if ph == 0:
                    tiles = [tv[table_s[0, GROUP * g + v]] for v in range(GROUP)]
                    left = jnp.concatenate([t[:, :half] for t in tiles], axis=1)
                    later[g] = jnp.concatenate([t[:, half:] for t in tiles], axis=1)
                else:
                    left = later[g]
                right = jnp.concatenate(
                    [recv[ph][table_s[1, GROUP * g + v]] for v in range(GROUP)], axis=0
                )
                prod = jnp.dot(left, right, preferred_element_type=jnp.float32)
                steps[g + 1] = jnp.where(table_s[2, g] == 1, steps[g], 0.0) + prod

    loops = (steps.shape[0] - 1) // UNROLL
    take(0, range(8))
    taken(0)
    fill.wait()
    products(0, 0, loops // 2)
    take(1, range(4))
    products(0, loops // 2, loops)
    for r in range(row_tiles):
        sums[r] = steps[table_s[3, r]]
    take(1, range(4, 8))
    taken(1)
    products(1, 0, loops)

    lanes = width // 2
    mine_cols = pl.ds(pl.multiple_of(core * lanes, lanes), lanes)
    sib_cols = pl.ds(pl.multiple_of((1 - core) * lanes, lanes), lanes)

    def swap(b):
        at = pl.ds(b * CHUNK, CHUNK)
        return pltpu.make_async_remote_copy(
            src_ref=part.at[at], dst_ref=other.at[at],
            send_sem=pssem.at[b], recv_sem=prsem.at[b],
            device_id=sib, device_id_type=MESH,
        )

    for b in range(row_tiles // CHUNK):
        for r in range(b * CHUNK, (b + 1) * CHUNK):
            part[r] = sums[r, :, sib_cols] + steps[table_s[3, r], :, sib_cols]
        swap(b).start()
    term[...] = jnp.zeros(term.shape, term.dtype)
    for b in range(row_tiles // CHUNK):
        swap(b).wait_recv()
        for r in range(b * CHUNK, (b + 1) * CHUNK):
            mine_sum = sums[r, :, mine_cols] + steps[table_s[3, r], :, mine_cols]
            mine_sum += other[r]
            agg[core, r * tile : (r + 1) * tile, :] = mine_sum.astype(jnp.bfloat16)
        left = jnp.concatenate([nft[b * CHUNK + v] for v in range(CHUNK)], axis=1)
        right = agg[core, b * CHUNK * tile : (b + 1) * CHUNK * tile, :]
        term[...] += jnp.dot(left, right, preferred_element_type=jnp.float32)

    odds = [lax.rem(v, 2) for v in (x, y, z)]
    ends = [lax.rem(lax.div(v + 1, 2), 2) for v in (x, y, z)]
    piece = red.shape[1]

    def rows_of(s):
        return pl.ds(pl.multiple_of(s * piece, piece), piece)

    def in_cube(n):
        bits = (n & 1, (n >> 1) & 1, n >> 2)
        px, py, pz = [v + b * (1 - 2 * o) for v, o, b in zip((x, y, z), odds, bits)]
        ox, oy, oz = [o + b * (1 - 2 * o) for o, b in zip(ends, bits)]
        return py * (SIDE * SIDE) + pz * SIDE + px, ox + 2 * oy + 4 * oz

    def facing(n):
        bits = (n & 1, (n >> 1) & 1, n >> 2)
        px, py, pz = [3 - v if b else v for v, b in zip((x, y, z), bits)]
        return py * (SIDE * SIDE) + pz * SIDE + px

    spot = in_cube(0)[1]
    cube = lax.div(x, 2) + 2 * lax.div(y, 2) + 4 * lax.div(z, 2)
    for n in range(1, 8):
        q, to = in_cube(n)
        pltpu.make_async_remote_copy(
            src_ref=term.at[rows_of(to)], dst_ref=red.at[n - 1],
            send_sem=r1s, recv_sem=r1r, device_id=(q, core), device_id_type=MESH,
        ).start()
    give = pltpu.make_async_remote_copy(
        src_ref=agg.at[core], dst_ref=agg.at[core],
        send_sem=r5s, recv_sem=r5r, device_id=sib, device_id_type=MESH,
    )
    give.start()
    mine_sum = term[rows_of(spot), :]
    first = wait_bytes(red, r1s, r1r)
    first.wait_recv()
    for n in range(7):
        mine_sum += red[n]
    line[cube] = mine_sum
    for n in range(1, 8):
        pltpu.make_async_remote_copy(
            src_ref=line.at[cube], dst_ref=line.at[cube],
            send_sem=r2s, recv_sem=r2r, device_id=(facing(n), core), device_id_type=MESH,
        ).start()

    give.wait_recv()

    @pl.loop(0, rows // 512)
    def _(b):
        at = pl.ds(pl.multiple_of(b * 512, 512), 512)
        total = sum(
            lax.dot_general(
                agg[h, at, :], wt[:, h * lanes : (h + 1) * lanes], (((1,), (1,)), ((), ())),
                preferred_element_type=jnp.float32,
            )
            for h in range(2)
        )
        ing[at, :] = total.astype(jnp.bfloat16)

    out_copy = pltpu.make_async_copy(ing, ing_hbm, out_sem.at[0])
    out_copy.start()
    second = wait_bytes(line.at[pl.ds(0, 7)], r2s, r2r)
    second.wait_recv()
    total = line[0]
    for n in range(1, 8):
        total += line[n]
    done[core, rows_of(spot), :] = total * jnp.float32(scale)
    for n in range(1, 8):
        pltpu.make_async_remote_copy(
            src_ref=done.at[core, rows_of(spot)], dst_ref=done.at[core, rows_of(spot)],
            send_sem=r3s, recv_sem=r3r, device_id=(in_cube(n)[0], core), device_id_type=MESH,
        ).start()
    for ph in range(2):
        wait_bytes(sbuf.at[ph, pl.ds(0, peers - 1)], ssem, ssem).wait_send()
        wait_bytes(sbuf.at[ph], fssem.at[ph], frsem.at[ph]).wait_send()
    for b in range(row_tiles // CHUNK):
        swap(b).wait_send()
    first.wait_send()
    second.wait_send()
    give.wait_send()
    third = wait_bytes(red, r3s, r3r)
    third.wait_recv()
    fourth = pltpu.make_async_remote_copy(
        src_ref=done.at[core], dst_ref=done.at[core],
        send_sem=r4s, recv_sem=r4r, device_id=sib, device_id_type=MESH,
    )
    fourth.start()
    mine_copy = pltpu.make_async_copy(done.at[core], wg_hbm.at[core], out_sem.at[1])
    mine_copy.start()
    third.wait_send()
    fourth.wait()
    sib_copy = pltpu.make_async_copy(done.at[1 - core], wg_hbm.at[1 - core], out_sem.at[2])
    sib_copy.start()
    out_copy.wait()
    mine_copy.wait()
    sib_copy.wait()


def finish_kernel(ing_in, wg_in, ing_out, wg_out, ing, wg, in_sem, out_sem):
    cuts = [
        (ing_in.at[at], ing.at[at], ing_out.at[at])
        for at in (pl.ds(n * 512, 512) for n in range(ing.shape[0] // 512))
    ]
    lanes = wg.shape[2]
    cuts += [
        (wg_in.at[h], wg.at[h], wg_out.at[:, pl.ds(h * lanes, lanes)]) for h in range(2)
    ]
    reads = [
        pltpu.make_async_copy(src, mid, in_sem.at[n])
        for n, (src, mid, _) in enumerate(cuts)
    ]
    writes = [
        pltpu.make_async_copy(mid, dst, out_sem.at[n])
        for n, (_, mid, dst) in enumerate(cuts)
    ]
    for read in reads:
        read.start()
    for read, write in zip(reads, writes):
        read.wait()
        write.start()
    for write in writes:
        write.wait()


def local(node_feats, out_grad, mask_bits, weight, send_rows, tile_vals, tile_row, tile_peer):
    rows, width = node_feats.shape
    peers, tile = send_rows.shape[1:]
    slots = tile_vals.shape[2]
    half = tile // 2
    row_tiles = rows // tile
    words = mask_bits.shape[1]
    most = -(-(slots + row_tiles * (GROUP - 1)) // GROUP)
    most = -(-most // UNROLL) * UNROLL
    places = -(-most * GROUP // 128) * 128
    piece = width // 8
    lanes = width // 2
    scale = 1.0 / math.sqrt(rows * lax.axis_size("row"))
    anywhere = pl.BlockSpec(memory_space=pl.ANY)
    bf16, f32, i32 = jnp.bfloat16, jnp.float32, jnp.int32
    dma = pltpu.SemaphoreType.DMA
    in_shape = jax.ShapeDtypeStruct((rows, width), bf16)
    parts = pl.pallas_call(
        lambda *refs: kernel(scale, *refs),
        out_shape=(in_shape, jax.ShapeDtypeStruct((2, width, lanes), f32)),
        in_specs=[anywhere] * 8,
        out_specs=(anywhere, anywhere),
        scratch_shapes=[
            pltpu.VMEM((rows, width), bf16),
            pltpu.VMEM((words, rows), i32),
            pltpu.VMEM((peers, tile), i32),
            pltpu.VMEM((1, slots), i32),
            pltpu.VMEM((1, slots), i32),
            pltpu.VMEM((rows, width), bf16),
            pltpu.VMEM((width, width), bf16),
            pltpu.VMEM((slots, tile, tile), bf16),
            pltpu.VMEM((rows, width), bf16),
            pltpu.VMEM((128, 128), i32),
            pltpu.VMEM((128, 128), i32),
            pltpu.VMEM((peers, half, 128), i32),
            pltpu.VMEM((4 * half, rows), bf16),
            pltpu.VMEM((2, peers, half // 2, width), bf16),
            pltpu.VMEM((peers + 1, half, width), bf16),
            pltpu.VMEM((peers + 1, half, width), bf16),
            pltpu.VMEM((8, places), i32),
            pltpu.SMEM((8, places), i32),
            pltpu.VMEM((most, tile, GROUP * half), bf16),
            pltpu.VMEM((most + 1, tile, width), f32),
            pltpu.VMEM((row_tiles, tile, width), f32),
            pltpu.VMEM((row_tiles, tile, lanes), f32),
            pltpu.VMEM((row_tiles, tile, lanes), f32),
            pltpu.VMEM((row_tiles, width, tile), bf16),
            pltpu.VMEM((rows, width), bf16),
            pltpu.VMEM((2, rows, lanes), bf16),
            pltpu.VMEM((width, lanes), f32),
            pltpu.VMEM((7, piece, lanes), f32),
            pltpu.VMEM((8, piece, lanes), f32),
            pltpu.VMEM((2, width, lanes), f32),
            dma((7,)), dma, dma, dma((2,)), dma((3,)),
            pltpu.SemaphoreType.REGULAR, dma, dma((16,)), dma((2,)), dma((2,)),
            dma((row_tiles // CHUNK,)), dma((row_tiles // CHUNK,)),
            dma, dma, dma, dma, dma, dma, dma, dma, dma, dma,
        ],
        compiler_params=pltpu.CompilerParams(
            collective_id=0, has_side_effects=True, vmem_limit_bytes=60 * 2**20
        ),
        name="layer",
    )(
        out_grad, mask_bits.T, send_rows[0], tile_row[0], tile_peer[0],
        node_feats, weight, tile_vals[0, 0],
    )
    return pl.pallas_call(
        finish_kernel,
        out_shape=(in_shape, jax.ShapeDtypeStruct((width, width), f32)),
        in_specs=[anywhere] * 2,
        out_specs=(anywhere, anywhere),
        scratch_shapes=[
            pltpu.VMEM((rows, width), bf16),
            pltpu.VMEM((2, width, lanes), f32),
            dma((rows // 512 + 2,)),
            dma((rows // 512 + 2,)),
        ],
        name="finish",
    )(*parts)


def solution(mesh):
    placed = (
        P("row", None),
        P("row", None),
        P("row", None),
        P(),
        P("row", None, None),
        P("row", "rep", None, None, None),
        P("row", "rep", None),
        P("row", "rep", None),
    )
    return jax.shard_map(
        local, mesh=mesh, in_specs=placed, out_specs=(P("row", None), P()), check_vma=False
    )
```

```python
import math

import jax
import jax.numpy as jnp
from jax import lax
from jax.experimental import pallas as pl
from jax.experimental.pallas import tpu as pltpu
from jax.sharding import PartitionSpec as P

MESH = pl.DeviceIdType.MESH
SIDE = 4
UORDER = (0, 7, 1, 6, 2, 5, 3, 4)
GROUP = 8
CHUNK = 4
UNROLL = 40
PLANE = [(0, a, b) for a in range(4) for b in range(4) if (a, b) != (0, 0)]
LINE = [(a, 0, 0) for a in range(1, 4)]


def ring(v):
    return [v] + [lax.rem(v + d, SIDE) for d in range(1, SIDE)]


def group_rows(i, x, y, z):
    g = 7 - i
    odd = (lax.rem(g, 2), lax.rem(lax.div(g, 2), 2), lax.div(g, 4))
    at = [
        [lax.rem(v + o, SIDE), lax.rem(v + o + 2, SIDE)]
        for v, o in zip((x, y, z), odd)
    ]
    return [
        at[1][(w >> 1) & 1] * (SIDE * SIDE) + at[2][w >> 2] * SIDE + at[0][w & 1] for w in UORDER
    ]


def iota(shape, dim):
    return lax.broadcasted_iota(jnp.int32, shape, dim)


def place_of(peer, x, y, z):
    dx, dy, dz = (x + 4 - (peer & 3)) & 3, (y + 4 - (peer >> 4)) & 3, (z + 4 - ((peer >> 2) & 3)) & 3
    g = (dx & 1) + 2 * (dy & 1) + 4 * (dz & 1)
    w = (dx >> 1) + 2 * (dy >> 1) + 4 * (dz >> 1)
    return 8 * (7 - g) + jnp.where(w < 4, 2 * w, 15 - 2 * w)


def layout_tables(row, peer, row_tiles, zero_peer, places):
    slots = row.shape[1]
    key = jnp.where(row < 0, row_tiles, row)
    key_down = jnp.broadcast_to(key, (128, slots)).T
    peer_down = jnp.broadcast_to(peer, (128, slots)).T
    down = iota((slots, 128), 0)
    across = iota((slots, 128), 1)
    count = jnp.sum((key_down == across).astype(jnp.int32), axis=0, keepdims=True)
    groups = jnp.where(iota((1, 128), 1) < row_tiles, (count + GROUP - 1) // GROUP, 0)
    groups_down = jnp.broadcast_to(groups, (128, 128)).T
    r_down, r_across = iota((128, 128), 0), iota((128, 128), 1)
    first = jnp.sum(jnp.where(r_down < r_across, groups_down, 0), axis=0, keepdims=True)
    first_down = jnp.broadcast_to(first, (128, 128)).T

    spots = []
    for b in range(slots // 128):
        key_here = key[:, b * 128 : (b + 1) * 128]
        before = (key_down == key_here) & (down < across + b * 128)
        rank = jnp.sum(before.astype(jnp.int32), axis=0, keepdims=True)
        base = jnp.sum(jnp.where(r_down < key_here, groups_down, 0), axis=0, keepdims=True)
        spots.append(jnp.where(key_here < row_tiles, base * GROUP + rank, -1))
    spot_down = jnp.broadcast_to(jnp.concatenate(spots, axis=1), (128, slots)).T

    slot_at, peer_at, goes_on = [], [], []
    for b in range(places // 128):
        hit = spot_down == across + b * 128
        slot_at.append(jnp.sum(jnp.where(hit, down, 0), axis=0, keepdims=True))
        peer_at.append(
            jnp.sum(jnp.where(hit, peer_down - zero_peer, 0), axis=0, keepdims=True) + zero_peer
        )
        opens = (first_down == r_across + b * 128) & (groups_down > 0)
        goes_on.append(1 - jnp.sum(opens.astype(jnp.int32), axis=0, keepdims=True))
    last = jnp.where(groups > 0, first + groups, 0)
    last = jnp.concatenate([last, jnp.zeros((1, places - 128), jnp.int32)], axis=1)
    rows = [jnp.concatenate(part, axis=1) for part in (slot_at, peer_at, goes_on)] + [last]
    return jnp.concatenate(rows + [jnp.zeros((8 - len(rows), places), jnp.int32)], axis=0)


def kernel(
    scale,
    og_hbm, mb_hbm, sr_hbm, row_hbm, peer_hbm, nf_hbm, wt_hbm, tv_hbm,
    ing_hbm, wg_hbm,
    og, mb, sr, row_v, peer_v, nf, wt, tv,
    gp, listed, turned, wide, hot, sbuf, recv_a, recv_b, table_v, table_s,
    later, steps, sums, part, other, nft, ing, agg, term, red, line, done,
    in_sem, tv_sem, table_sem, own_sem, out_sem,
    near_sem, ssem, rsem, fssem, frsem, pssem, prsem, r1s, r1r, r2s, r2r, r3s, r3r, r4s, r4r, r5s, r5r,
):
    me = lax.axis_index("row")
    core = lax.axis_index("rep")
    x, z, y = lax.rem(me, SIDE), lax.rem(lax.div(me, SIDE), SIDE), lax.div(me, SIDE * SIDE)
    xs, ys, zs = ring(x), ring(y), ring(z)

    def shifted(off):
        return ys[off[1]] * (SIDE * SIDE) + zs[off[2]] * SIDE + xs[off[0]]

    rows, width = gp.shape
    peers, quarter = sbuf.shape[1:3]
    half = 2 * quarter
    tile = 2 * half
    recv = (recv_a, recv_b)
    row_tiles = rows // tile
    sib = (me, 1 - core)

    loads = [
        pltpu.make_async_copy(src, dst, in_sem.at[n])
        for n, (src, dst) in enumerate(
            (
                (sr_hbm, sr), (mb_hbm, mb), (og_hbm, og), (row_hbm, row_v),
                (peer_hbm, peer_v), (nf_hbm, nf), (wt_hbm, wt),
            )
        )
    ]
    for load in loads[:5]:
        load.start()

    barrier = pltpu.get_barrier_semaphore()
    pl.semaphore_signal(barrier, inc=1, device_id=sib, device_id_type=MESH)
    for off in LINE + PLANE:
        pl.semaphore_signal(
            barrier, inc=1, device_id=(shifted(off), core), device_id_type=MESH
        )
    greeted = 1 + len(LINE) + len(PLANE)

    loads[0].wait()
    listed[...] = jnp.full(listed.shape, -1, jnp.int32)

    @pl.loop(0, 8)
    def _(i):
        for u, q in enumerate(group_rows(i, x, y, z)):
            listed[pl.ds(i * 8 + u, 1), :] = sr[pl.ds(q, 1), :]

    turned[...] = listed[...].T
    mine = jnp.concatenate(
        [
            turned[pl.ds(pl.multiple_of(ph * half + core * quarter, quarter), quarter), :]
            for ph in range(2)
        ],
        axis=0,
    )
    for j in range(64):
        wide[j] = jnp.broadcast_to(mine[:, j : j + 1], (half, 128))

    pl.semaphore_wait(barrier, greeted)
    for off in LINE:
        pl.semaphore_signal(
            near_sem, inc=1, device_id=(shifted(off), core), device_id_type=MESH
        )

    words = mb.shape[0]
    feature = iota((2 * words, width), 1)
    byte_at = iota((2 * words, width), 0)
    spread = (feature // 16 == byte_at % words) & ((feature % 16 >= 8) == (byte_at >= words))
    spread = jnp.where(spread, 1.0, 0.0).astype(jnp.bfloat16)
    step = 256
    bit = iota((step, width), 1) % 8
    loads[1].wait()
    loads[2].wait()

    @pl.loop(0, rows // step)
    def _(b):
        at = pl.ds(pl.multiple_of(b * step, step), step)
        bits = mb[:, at]
        both = jnp.concatenate([bits & 255, bits >> 8], axis=0)
        both = both.astype(jnp.float32).astype(jnp.bfloat16)
        byte = lax.dot_general(
            both, spread, (((0,), (0,)), ((), ())), preferred_element_type=jnp.float32
        )
        keep = (byte.astype(jnp.int32) >> bit) & 1
        grad = og[at, :].astype(jnp.float32)
        gp[at, :] = jnp.where(keep == 1, grad, 0.0).astype(jnp.bfloat16)

    lane = iota((quarter, 128), 1)
    mine_rows = pl.ds(pl.multiple_of(core * quarter, quarter), quarter)

    def send(ph, t, u, q):
        return pltpu.make_async_remote_copy(
            src_ref=sbuf.at[ph, (t - 8 * ph) * 8 + u],
            dst_ref=recv[ph].at[(t - 8 * ph) * 8 + u, mine_rows],
            send_sem=ssem, recv_sem=rsem.at[t],
            device_id=(q, core), device_id_type=MESH,
        )

    def wait_bytes(like, send_sem, recv_sem):
        return pltpu.make_async_remote_copy(
            src_ref=like, dst_ref=like, send_sem=send_sem, recv_sem=recv_sem,
            device_id=sib, device_id_type=MESH,
        )

    def keep_own(ph):
        return pltpu.make_async_copy(
            sbuf.at[ph, peers - 8], recv[ph].at[peers - 8, mine_rows], own_sem.at[ph]
        )

    for ph in range(2):

        @pl.loop(8 * ph, 8 * ph + 8)
        def _(t, ph=ph):
            i = t - 8 * ph
            ahead = group_rows(i, x, y, z)
            for u in range(8):
                listed_at = wide[i * 8 + u, ph * quarter : (ph + 1) * quarter]
                block = listed_at >> 7
                one = jnp.where((listed_at & 127) == lane, 1.0, 0.0)
                for c in range(rows // 128):
                    hot[u * quarter : (u + 1) * quarter, c * 128 : (c + 1) * 128] = jnp.where(
                        block == c, one, 0.0
                    ).astype(jnp.bfloat16)
            picked = jnp.dot(hot[...], gp[...], preferred_element_type=jnp.float32)
            for u in range(8):
                sbuf[ph, i * 8 + u] = picked[u * quarter : (u + 1) * quarter].astype(jnp.bfloat16)

            @pl.when(t == 0)
            def _():
                pl.semaphore_wait(near_sem, len(LINE))

            @pl.when(i < 7)
            def _():
                send(ph, t, 0, ahead[0]).start()

            @pl.when(i == 7)
            def _():
                keep_own(ph).start()

            for u in range(1, 8):
                send(ph, t, u, ahead[u]).start()

    fill = pltpu.make_async_copy(tv_hbm, tv, tv_sem)
    fill.start()
    for load in loads[5:]:
        load.start()
    loads[3].wait()
    loads[4].wait()
    table_v[...] = layout_tables(
        row_v[...], place_of(peer_v[...], x, y, z), row_tiles, peers, table_v.shape[1]
    )
    table_copy = pltpu.make_async_copy(table_v, table_s, table_sem)
    table_copy.start()
    for buf in recv:
        buf[peers] = jnp.zeros(buf.shape[1:], buf.dtype)
    steps[0] = jnp.zeros(steps.shape[1:], steps.dtype)
    loads[5].wait()
    loads[6].wait()

    @pl.loop(0, row_tiles)
    def _(r):
        at = pl.ds(pl.multiple_of(r * tile, tile), tile)
        nft[r] = nf[at, :].T

    table_copy.wait()

    def take(ph, groups):
        for i in groups:
            lists = 8 if i < 7 else 7
            wait_bytes(sbuf.at[0, pl.ds(0, lists)], ssem, rsem.at[8 * ph + i]).wait_recv()
            if i == 7:
                keep_own(ph).wait()
            here = recv[ph].at[pl.ds(i * 8, 8), mine_rows]
            pltpu.make_async_remote_copy(
                src_ref=here, dst_ref=here, send_sem=fssem.at[ph], recv_sem=frsem.at[ph],
                device_id=sib, device_id_type=MESH,
            ).start()

    def taken(ph):
        wait_bytes(sbuf.at[0], fssem.at[ph], frsem.at[ph]).wait_recv()

    def products(ph, start, stop):
        @pl.loop(start, stop)
        def _(i):
            for n in range(UNROLL):
                g = i * UNROLL + n
                if ph == 0:
                    tiles = [tv[table_s[0, GROUP * g + v]] for v in range(GROUP)]
                    left = jnp.concatenate([t[:, :half] for t in tiles], axis=1)
                    later[g] = jnp.concatenate([t[:, half:] for t in tiles], axis=1)
                else:
                    left = later[g]
                right = jnp.concatenate(
                    [recv[ph][table_s[1, GROUP * g + v]] for v in range(GROUP)], axis=0
                )
                prod = jnp.dot(left, right, preferred_element_type=jnp.float32)
                steps[g + 1] = jnp.where(table_s[2, g] == 1, steps[g], 0.0) + prod

    loops = (steps.shape[0] - 1) // UNROLL
    take(0, range(8))
    taken(0)
    fill.wait()
    products(0, 0, loops // 2)
    take(1, range(4))
    products(0, loops // 2, loops)
    for r in range(row_tiles):
        sums[r] = steps[table_s[3, r]]
    take(1, range(4, 8))
    taken(1)
    products(1, 0, loops)

    lanes = width // 2
    mine_cols = pl.ds(pl.multiple_of(core * lanes, lanes), lanes)
    sib_cols = pl.ds(pl.multiple_of((1 - core) * lanes, lanes), lanes)

    def swap(b):
        at = pl.ds(b * CHUNK, CHUNK)
        return pltpu.make_async_remote_copy(
            src_ref=part.at[at], dst_ref=other.at[at],
            send_sem=pssem.at[b], recv_sem=prsem.at[b],
            device_id=sib, device_id_type=MESH,
        )

    for b in range(row_tiles // CHUNK):
        for r in range(b * CHUNK, (b + 1) * CHUNK):
            part[r] = sums[r, :, sib_cols] + steps[table_s[3, r], :, sib_cols]
        swap(b).start()
    term[...] = jnp.zeros(term.shape, term.dtype)
    for b in range(row_tiles // CHUNK):
        swap(b).wait_recv()
        for r in range(b * CHUNK, (b + 1) * CHUNK):
            mine_sum = sums[r, :, mine_cols] + steps[table_s[3, r], :, mine_cols]
            mine_sum += other[r]
            agg[core, r * tile : (r + 1) * tile, :] = mine_sum.astype(jnp.bfloat16)
        left = jnp.concatenate([nft[b * CHUNK + v] for v in range(CHUNK)], axis=1)
        right = agg[core, b * CHUNK * tile : (b + 1) * CHUNK * tile, :]
        term[...] += jnp.dot(left, right, preferred_element_type=jnp.float32)

    odds = [lax.rem(v, 2) for v in (x, y, z)]
    ends = [lax.rem(lax.div(v + 1, 2), 2) for v in (x, y, z)]
    piece = red.shape[1]

    def rows_of(s):
        return pl.ds(pl.multiple_of(s * piece, piece), piece)

    def in_cube(n):
        bits = (n & 1, (n >> 1) & 1, n >> 2)
        px, py, pz = [v + b * (1 - 2 * o) for v, o, b in zip((x, y, z), odds, bits)]
        ox, oy, oz = [o + b * (1 - 2 * o) for o, b in zip(ends, bits)]
        return py * (SIDE * SIDE) + pz * SIDE + px, ox + 2 * oy + 4 * oz

    def facing(n):
        bits = (n & 1, (n >> 1) & 1, n >> 2)
        px, py, pz = [3 - v if b else v for v, b in zip((x, y, z), bits)]
        return py * (SIDE * SIDE) + pz * SIDE + px

    spot = in_cube(0)[1]
    cube = lax.div(x, 2) + 2 * lax.div(y, 2) + 4 * lax.div(z, 2)
    for n in range(1, 8):
        q, to = in_cube(n)
        pltpu.make_async_remote_copy(
            src_ref=term.at[rows_of(to)], dst_ref=red.at[n - 1],
            send_sem=r1s, recv_sem=r1r, device_id=(q, core), device_id_type=MESH,
        ).start()
    give = pltpu.make_async_remote_copy(
        src_ref=agg.at[core], dst_ref=agg.at[core],
        send_sem=r5s, recv_sem=r5r, device_id=sib, device_id_type=MESH,
    )
    give.start()
    mine_sum = term[rows_of(spot), :]
    first = wait_bytes(red, r1s, r1r)
    first.wait_recv()
    for n in range(7):
        mine_sum += red[n]
    line[cube] = mine_sum
    for n in range(1, 8):
        pltpu.make_async_remote_copy(
            src_ref=line.at[cube], dst_ref=line.at[cube],
            send_sem=r2s, recv_sem=r2r, device_id=(facing(n), core), device_id_type=MESH,
        ).start()

    give.wait_recv()

    @pl.loop(0, rows // 512)
    def _(b):
        at = pl.ds(pl.multiple_of(b * 512, 512), 512)
        total = sum(
            lax.dot_general(
                agg[h, at, :], wt[:, h * lanes : (h + 1) * lanes], (((1,), (1,)), ((), ())),
                preferred_element_type=jnp.float32,
            )
            for h in range(2)
        )
        ing[at, :] = total.astype(jnp.bfloat16)

    out_copy = pltpu.make_async_copy(ing, ing_hbm, out_sem.at[0])
    out_copy.start()
    second = wait_bytes(line.at[pl.ds(0, 7)], r2s, r2r)
    second.wait_recv()
    total = line[0]
    for n in range(1, 8):
        total += line[n]
    done[core, rows_of(spot), :] = total * jnp.float32(scale)
    def hand_out(to, send_sem, recv_sem):
        here = done.at[core, rows_of(spot)]
        pltpu.make_async_remote_copy(
            src_ref=here, dst_ref=here, send_sem=send_sem, recv_sem=recv_sem,
            device_id=to, device_id_type=MESH,
        ).start()

    for n in range(1, 8):
        hand_out((in_cube(n)[0], core), r3s, r3r)
        hand_out((in_cube(n)[0], 1 - core), r4s, r4r)
    hand_out(sib, r4s, r4r)
    for ph in range(2):
        wait_bytes(sbuf.at[ph, pl.ds(0, peers - 1)], ssem, ssem).wait_send()
        wait_bytes(sbuf.at[ph], fssem.at[ph], frsem.at[ph]).wait_send()
    for b in range(row_tiles // CHUNK):
        swap(b).wait_send()
    first.wait_send()
    second.wait_send()
    give.wait_send()
    third = wait_bytes(red, r3s, r3r)
    third.wait_recv()
    fourth = wait_bytes(line, r4s, r4r)
    mine_copy = pltpu.make_async_copy(done.at[core], wg_hbm.at[core], out_sem.at[1])
    mine_copy.start()
    third.wait_send()
    fourth.wait()
    sib_copy = pltpu.make_async_copy(done.at[1 - core], wg_hbm.at[1 - core], out_sem.at[2])
    sib_copy.start()
    out_copy.wait()
    mine_copy.wait()
    sib_copy.wait()


def finish_kernel(ing_in, wg_in, ing_out, wg_out, ing, wg, in_sem, out_sem):
    cuts = [
        (ing_in.at[at], ing.at[at], ing_out.at[at])
        for at in (pl.ds(n * 512, 512) for n in range(ing.shape[0] // 512))
    ]
    lanes = wg.shape[2]
    cuts += [
        (wg_in.at[h], wg.at[h], wg_out.at[:, pl.ds(h * lanes, lanes)]) for h in range(2)
    ]
    reads = [
        pltpu.make_async_copy(src, mid, in_sem.at[n])
        for n, (src, mid, _) in enumerate(cuts)
    ]
    writes = [
        pltpu.make_async_copy(mid, dst, out_sem.at[n])
        for n, (_, mid, dst) in enumerate(cuts)
    ]
    for read in reads:
        read.start()
    for read, write in zip(reads, writes):
        read.wait()
        write.start()
    for write in writes:
        write.wait()


def local(node_feats, out_grad, mask_bits, weight, send_rows, tile_vals, tile_row, tile_peer):
    rows, width = node_feats.shape
    peers, tile = send_rows.shape[1:]
    slots = tile_vals.shape[2]
    half = tile // 2
    row_tiles = rows // tile
    words = mask_bits.shape[1]
    most = -(-(slots + row_tiles * (GROUP - 1)) // GROUP)
    most = -(-most // UNROLL) * UNROLL
    places = -(-most * GROUP // 128) * 128
    piece = width // 8
    lanes = width // 2
    scale = 1.0 / math.sqrt(rows * lax.axis_size("row"))
    anywhere = pl.BlockSpec(memory_space=pl.ANY)
    bf16, f32, i32 = jnp.bfloat16, jnp.float32, jnp.int32
    dma = pltpu.SemaphoreType.DMA
    in_shape = jax.ShapeDtypeStruct((rows, width), bf16)
    parts = pl.pallas_call(
        lambda *refs: kernel(scale, *refs),
        out_shape=(in_shape, jax.ShapeDtypeStruct((2, width, lanes), f32)),
        in_specs=[anywhere] * 8,
        out_specs=(anywhere, anywhere),
        scratch_shapes=[
            pltpu.VMEM((rows, width), bf16),
            pltpu.VMEM((words, rows), i32),
            pltpu.VMEM((peers, tile), i32),
            pltpu.VMEM((1, slots), i32),
            pltpu.VMEM((1, slots), i32),
            pltpu.VMEM((rows, width), bf16),
            pltpu.VMEM((width, width), bf16),
            pltpu.VMEM((slots, tile, tile), bf16),
            pltpu.VMEM((rows, width), bf16),
            pltpu.VMEM((128, 128), i32),
            pltpu.VMEM((128, 128), i32),
            pltpu.VMEM((peers, half, 128), i32),
            pltpu.VMEM((4 * half, rows), bf16),
            pltpu.VMEM((2, peers, half // 2, width), bf16),
            pltpu.VMEM((peers + 1, half, width), bf16),
            pltpu.VMEM((peers + 1, half, width), bf16),
            pltpu.VMEM((8, places), i32),
            pltpu.SMEM((8, places), i32),
            pltpu.VMEM((most, tile, GROUP * half), bf16),
            pltpu.VMEM((most + 1, tile, width), f32),
            pltpu.VMEM((row_tiles, tile, width), f32),
            pltpu.VMEM((row_tiles, tile, lanes), f32),
            pltpu.VMEM((row_tiles, tile, lanes), f32),
            pltpu.VMEM((row_tiles, width, tile), bf16),
            pltpu.VMEM((rows, width), bf16),
            pltpu.VMEM((2, rows, lanes), bf16),
            pltpu.VMEM((width, lanes), f32),
            pltpu.VMEM((7, piece, lanes), f32),
            pltpu.VMEM((8, piece, lanes), f32),
            pltpu.VMEM((2, width, lanes), f32),
            dma((7,)), dma, dma, dma((2,)), dma((3,)),
            pltpu.SemaphoreType.REGULAR, dma, dma((16,)), dma((2,)), dma((2,)),
            dma((row_tiles // CHUNK,)), dma((row_tiles // CHUNK,)),
            dma, dma, dma, dma, dma, dma, dma, dma, dma, dma,
        ],
        compiler_params=pltpu.CompilerParams(
            collective_id=0, has_side_effects=True, vmem_limit_bytes=60 * 2**20
        ),
        name="layer",
    )(
        out_grad, mask_bits.T, send_rows[0], tile_row[0], tile_peer[0],
        node_feats, weight, tile_vals[0, 0],
    )
    return pl.pallas_call(
        finish_kernel,
        out_shape=(in_shape, jax.ShapeDtypeStruct((width, width), f32)),
        in_specs=[anywhere] * 2,
        out_specs=(anywhere, anywhere),
        scratch_shapes=[
            pltpu.VMEM((rows, width), bf16),
            pltpu.VMEM((2, width, lanes), f32),
            dma((rows // 512 + 2,)),
            dma((rows // 512 + 2,)),
        ],
        name="finish",
    )(*parts)


def solution(mesh):
    placed = (
        P("row", None),
        P("row", None),
        P("row", None),
        P(),
        P("row", None, None),
        P("row", "rep", None, None, None),
        P("row", "rep", None),
        P("row", "rep", None),
    )
    return jax.shard_map(
        local, mesh=mesh, in_specs=placed, out_specs=(P("row", None), P()), check_vma=False
    )
```

```python
import math

import jax
import jax.numpy as jnp
from jax import lax
from jax.experimental import pallas as pl
from jax.experimental.pallas import tpu as pltpu
from jax.sharding import PartitionSpec as P

MESH = pl.DeviceIdType.MESH
SIDE = 4
UORDER = (0, 7, 1, 6, 2, 5, 3, 4)
GROUP = 8
CHUNK = 4
UNROLL = 40
PLANE = [(0, a, b) for a in range(4) for b in range(4) if (a, b) != (0, 0)]
LINE = [(a, 0, 0) for a in range(1, 4)]
FAR_FIRST = (7, 6, 5, 3, 4, 2, 1)


def ring(v):
    return [v] + [lax.rem(v + d, SIDE) for d in range(1, SIDE)]


def group_rows(i, x, y, z):
    g = 7 - i
    odd = (lax.rem(g, 2), lax.rem(lax.div(g, 2), 2), lax.div(g, 4))
    at = [
        [lax.rem(v + o, SIDE), lax.rem(v + o + 2, SIDE)]
        for v, o in zip((x, y, z), odd)
    ]
    return [
        at[1][(w >> 1) & 1] * (SIDE * SIDE) + at[2][w >> 2] * SIDE + at[0][w & 1] for w in UORDER
    ]


def iota(shape, dim):
    return lax.broadcasted_iota(jnp.int32, shape, dim)


def place_of(peer, x, y, z):
    dx, dy, dz = (x + 4 - (peer & 3)) & 3, (y + 4 - (peer >> 4)) & 3, (z + 4 - ((peer >> 2) & 3)) & 3
    g = (dx & 1) + 2 * (dy & 1) + 4 * (dz & 1)
    w = (dx >> 1) + 2 * (dy >> 1) + 4 * (dz >> 1)
    return 8 * (7 - g) + jnp.where(w < 4, 2 * w, 15 - 2 * w)


def layout_tables(row, peer, row_tiles, zero_peer, places):
    slots = row.shape[1]
    key = jnp.where(row < 0, row_tiles, row)
    key_down = jnp.broadcast_to(key, (128, slots)).T
    peer_down = jnp.broadcast_to(peer, (128, slots)).T
    down = iota((slots, 128), 0)
    across = iota((slots, 128), 1)
    count = jnp.sum((key_down == across).astype(jnp.int32), axis=0, keepdims=True)
    groups = jnp.where(iota((1, 128), 1) < row_tiles, (count + GROUP - 1) // GROUP, 0)
    groups_down = jnp.broadcast_to(groups, (128, 128)).T
    r_down, r_across = iota((128, 128), 0), iota((128, 128), 1)
    first = jnp.sum(jnp.where(r_down < r_across, groups_down, 0), axis=0, keepdims=True)
    first_down = jnp.broadcast_to(first, (128, 128)).T

    spots = []
    for b in range(slots // 128):
        key_here = key[:, b * 128 : (b + 1) * 128]
        before = (key_down == key_here) & (down < across + b * 128)
        rank = jnp.sum(before.astype(jnp.int32), axis=0, keepdims=True)
        base = jnp.sum(jnp.where(r_down < key_here, groups_down, 0), axis=0, keepdims=True)
        spots.append(jnp.where(key_here < row_tiles, base * GROUP + rank, -1))
    spot_down = jnp.broadcast_to(jnp.concatenate(spots, axis=1), (128, slots)).T

    slot_at, peer_at, goes_on = [], [], []
    for b in range(places // 128):
        hit = spot_down == across + b * 128
        slot_at.append(jnp.sum(jnp.where(hit, down, 0), axis=0, keepdims=True))
        peer_at.append(
            jnp.sum(jnp.where(hit, peer_down - zero_peer, 0), axis=0, keepdims=True) + zero_peer
        )
        opens = (first_down == r_across + b * 128) & (groups_down > 0)
        goes_on.append(1 - jnp.sum(opens.astype(jnp.int32), axis=0, keepdims=True))
    last = jnp.where(groups > 0, first + groups, 0)
    last = jnp.concatenate([last, jnp.zeros((1, places - 128), jnp.int32)], axis=1)
    rows = [jnp.concatenate(part, axis=1) for part in (slot_at, peer_at, goes_on)] + [last]
    return jnp.concatenate(rows + [jnp.zeros((8 - len(rows), places), jnp.int32)], axis=0)


def kernel(
    scale,
    og_hbm, mb_hbm, sr_hbm, row_hbm, peer_hbm, nf_hbm, wt_hbm, tv_hbm,
    ing_hbm, wg_hbm,
    og, mb, sr, row_v, peer_v, nf, wt, tv,
    gp, listed, turned, wide, hot, sbuf, recv_a, recv_b, table_v, table_s,
    later, steps, sums, part, other, nft, ing, agg, term, red, line, done,
    in_sem, tv_sem, table_sem, own_sem, out_sem,
    near_sem, ssem, rsem, fssem, frsem, pssem, prsem, r1s, r1r, r2s, r2r, r3s, r3r, r4s, r4r, r5s, r5r,
):
    me = lax.axis_index("row")
    core = lax.axis_index("rep")
    x, z, y = lax.rem(me, SIDE), lax.rem(lax.div(me, SIDE), SIDE), lax.div(me, SIDE * SIDE)
    xs, ys, zs = ring(x), ring(y), ring(z)

    def shifted(off):
        return ys[off[1]] * (SIDE * SIDE) + zs[off[2]] * SIDE + xs[off[0]]

    rows, width = gp.shape
    peers, quarter = sbuf.shape[1:3]
    half = 2 * quarter
    tile = 2 * half
    recv = (recv_a, recv_b)
    row_tiles = rows // tile
    sib = (me, 1 - core)

    loads = [
        pltpu.make_async_copy(src, dst, in_sem.at[n])
        for n, (src, dst) in enumerate(
            (
                (sr_hbm, sr), (mb_hbm, mb), (og_hbm, og), (row_hbm, row_v),
                (peer_hbm, peer_v), (nf_hbm, nf), (wt_hbm, wt),
            )
        )
    ]
    for load in loads[:5]:
        load.start()

    barrier = pltpu.get_barrier_semaphore()
    pl.semaphore_signal(barrier, inc=1, device_id=sib, device_id_type=MESH)
    for off in LINE + PLANE:
        pl.semaphore_signal(
            barrier, inc=1, device_id=(shifted(off), core), device_id_type=MESH
        )
    greeted = 1 + len(LINE) + len(PLANE)

    loads[0].wait()
    listed[...] = jnp.full(listed.shape, -1, jnp.int32)

    @pl.loop(0, 8)
    def _(i):
        for u, q in enumerate(group_rows(i, x, y, z)):
            listed[pl.ds(i * 8 + u, 1), :] = sr[pl.ds(q, 1), :]

    turned[...] = listed[...].T
    mine = jnp.concatenate(
        [
            turned[pl.ds(pl.multiple_of(ph * half + core * quarter, quarter), quarter), :]
            for ph in range(2)
        ],
        axis=0,
    )
    for j in range(64):
        wide[j] = jnp.broadcast_to(mine[:, j : j + 1], (half, 128))

    pl.semaphore_wait(barrier, greeted)
    for off in LINE:
        pl.semaphore_signal(
            near_sem, inc=1, device_id=(shifted(off), core), device_id_type=MESH
        )

    words = mb.shape[0]
    feature = iota((2 * words, width), 1)
    byte_at = iota((2 * words, width), 0)
    spread = (feature // 16 == byte_at % words) & ((feature % 16 >= 8) == (byte_at >= words))
    spread = jnp.where(spread, 1.0, 0.0).astype(jnp.bfloat16)
    step = 256
    bit = iota((step, width), 1) % 8
    loads[1].wait()
    loads[2].wait()

    @pl.loop(0, rows // step)
    def _(b):
        at = pl.ds(pl.multiple_of(b * step, step), step)
        bits = mb[:, at]
        both = jnp.concatenate([bits & 255, bits >> 8], axis=0)
        both = both.astype(jnp.float32).astype(jnp.bfloat16)
        byte = lax.dot_general(
            both, spread, (((0,), (0,)), ((), ())), preferred_element_type=jnp.float32
        )
        keep = (byte.astype(jnp.int32) >> bit) & 1
        grad = og[at, :].astype(jnp.float32)
        gp[at, :] = jnp.where(keep == 1, grad, 0.0).astype(jnp.bfloat16)

    lane = iota((quarter, 128), 1)
    mine_rows = pl.ds(pl.multiple_of(core * quarter, quarter), quarter)

    def send(ph, t, u, q):
        return pltpu.make_async_remote_copy(
            src_ref=sbuf.at[ph, (t - 8 * ph) * 8 + u],
            dst_ref=recv[ph].at[(t - 8 * ph) * 8 + u, mine_rows],
            send_sem=ssem, recv_sem=rsem.at[t],
            device_id=(q, core), device_id_type=MESH,
        )

    def wait_bytes(like, send_sem, recv_sem):
        return pltpu.make_async_remote_copy(
            src_ref=like, dst_ref=like, send_sem=send_sem, recv_sem=recv_sem,
            device_id=sib, device_id_type=MESH,
        )

    def keep_own(ph):
        return pltpu.make_async_copy(
            sbuf.at[ph, peers - 8], recv[ph].at[peers - 8, mine_rows], own_sem.at[ph]
        )

    for ph in range(2):

        @pl.loop(8 * ph, 8 * ph + 8)
        def _(t, ph=ph):
            i = t - 8 * ph
            ahead = group_rows(i, x, y, z)
            for u in range(8):
                listed_at = wide[i * 8 + u, ph * quarter : (ph + 1) * quarter]
                block = listed_at >> 7
                one = jnp.where((listed_at & 127) == lane, 1.0, 0.0)
                for c in range(rows // 128):
                    hot[u * quarter : (u + 1) * quarter, c * 128 : (c + 1) * 128] = jnp.where(
                        block == c, one, 0.0
                    ).astype(jnp.bfloat16)
            picked = jnp.dot(hot[...], gp[...], preferred_element_type=jnp.float32)
            for u in range(8):
                sbuf[ph, i * 8 + u] = picked[u * quarter : (u + 1) * quarter].astype(jnp.bfloat16)

            @pl.when(t == 0)
            def _():
                pl.semaphore_wait(near_sem, len(LINE))

            @pl.when(i < 7)
            def _():
                send(ph, t, 0, ahead[0]).start()

            @pl.when(i == 7)
            def _():
                keep_own(ph).start()

            for u in range(1, 8):
                send(ph, t, u, ahead[u]).start()

    fill = pltpu.make_async_copy(tv_hbm, tv, tv_sem)
    fill.start()
    for load in loads[5:]:
        load.start()
    loads[3].wait()
    loads[4].wait()
    table_v[...] = layout_tables(
        row_v[...], place_of(peer_v[...], x, y, z), row_tiles, peers, table_v.shape[1]
    )
    table_copy = pltpu.make_async_copy(table_v, table_s, table_sem)
    table_copy.start()
    for buf in recv:
        buf[peers] = jnp.zeros(buf.shape[1:], buf.dtype)
    steps[0] = jnp.zeros(steps.shape[1:], steps.dtype)
    loads[5].wait()
    loads[6].wait()

    @pl.loop(0, row_tiles)
    def _(r):
        at = pl.ds(pl.multiple_of(r * tile, tile), tile)
        nft[r] = nf[at, :].T

    table_copy.wait()

    def take(ph, groups):
        for i in groups:
            lists = 8 if i < 7 else 7
            wait_bytes(sbuf.at[0, pl.ds(0, lists)], ssem, rsem.at[8 * ph + i]).wait_recv()
            if i == 7:
                keep_own(ph).wait()
            here = recv[ph].at[pl.ds(i * 8, 8), mine_rows]
            pltpu.make_async_remote_copy(
                src_ref=here, dst_ref=here, send_sem=fssem.at[ph], recv_sem=frsem.at[ph],
                device_id=sib, device_id_type=MESH,
            ).start()

    def taken(ph):
        wait_bytes(sbuf.at[0], fssem.at[ph], frsem.at[ph]).wait_recv()

    def products(ph, start, stop):
        @pl.loop(start, stop)
        def _(i):
            for n in range(UNROLL):
                g = i * UNROLL + n
                if ph == 0:
                    tiles = [tv[table_s[0, GROUP * g + v]] for v in range(GROUP)]
                    left = jnp.concatenate([t[:, :half] for t in tiles], axis=1)
                    later[g] = jnp.concatenate([t[:, half:] for t in tiles], axis=1)
                else:
                    left = later[g]
                right = jnp.concatenate(
                    [recv[ph][table_s[1, GROUP * g + v]] for v in range(GROUP)], axis=0
                )
                prod = jnp.dot(left, right, preferred_element_type=jnp.float32)
                steps[g + 1] = jnp.where(table_s[2, g] == 1, steps[g], 0.0) + prod

    loops = (steps.shape[0] - 1) // UNROLL
    take(0, range(8))
    taken(0)
    fill.wait()
    products(0, 0, loops // 2)
    take(1, range(4))
    products(0, loops // 2, loops)
    for r in range(row_tiles):
        sums[r] = steps[table_s[3, r]]
    take(1, range(4, 8))
    taken(1)
    products(1, 0, loops)

    lanes = width // 2
    mine_cols = pl.ds(pl.multiple_of(core * lanes, lanes), lanes)
    sib_cols = pl.ds(pl.multiple_of((1 - core) * lanes, lanes), lanes)

    def swap(b):
        at = pl.ds(b * CHUNK, CHUNK)
        return pltpu.make_async_remote_copy(
            src_ref=part.at[at], dst_ref=other.at[at],
            send_sem=pssem.at[b], recv_sem=prsem.at[b],
            device_id=sib, device_id_type=MESH,
        )

    for b in range(row_tiles // CHUNK):
        for r in range(b * CHUNK, (b + 1) * CHUNK):
            part[r] = sums[r, :, sib_cols] + steps[table_s[3, r], :, sib_cols]
        swap(b).start()
    term[...] = jnp.zeros(term.shape, term.dtype)
    for b in range(row_tiles // CHUNK):
        swap(b).wait_recv()
        for r in range(b * CHUNK, (b + 1) * CHUNK):
            mine_sum = sums[r, :, mine_cols] + steps[table_s[3, r], :, mine_cols]
            mine_sum += other[r]
            agg[core, r * tile : (r + 1) * tile, :] = mine_sum.astype(jnp.bfloat16)
        left = jnp.concatenate([nft[b * CHUNK + v] for v in range(CHUNK)], axis=1)
        right = agg[core, b * CHUNK * tile : (b + 1) * CHUNK * tile, :]
        term[...] += jnp.dot(left, right, preferred_element_type=jnp.float32)

    odds = [lax.rem(v, 2) for v in (x, y, z)]
    ends = [lax.rem(lax.div(v + 1, 2), 2) for v in (x, y, z)]
    piece = red.shape[1]

    def rows_of(s):
        return pl.ds(pl.multiple_of(s * piece, piece), piece)

    def in_cube(n):
        bits = (n & 1, (n >> 1) & 1, n >> 2)
        px, py, pz = [v + b * (1 - 2 * o) for v, o, b in zip((x, y, z), odds, bits)]
        ox, oy, oz = [o + b * (1 - 2 * o) for o, b in zip(ends, bits)]
        return py * (SIDE * SIDE) + pz * SIDE + px, ox + 2 * oy + 4 * oz

    def facing(n):
        bits = (n & 1, (n >> 1) & 1, n >> 2)
        px, py, pz = [3 - v if b else v for v, b in zip((x, y, z), bits)]
        return py * (SIDE * SIDE) + pz * SIDE + px

    spot = in_cube(0)[1]
    cube = lax.div(x, 2) + 2 * lax.div(y, 2) + 4 * lax.div(z, 2)
    for n in FAR_FIRST:
        q, to = in_cube(n)
        pltpu.make_async_remote_copy(
            src_ref=term.at[rows_of(to)], dst_ref=red.at[n - 1],
            send_sem=r1s, recv_sem=r1r, device_id=(q, core), device_id_type=MESH,
        ).start()
    give = pltpu.make_async_remote_copy(
        src_ref=agg.at[core], dst_ref=agg.at[core],
        send_sem=r5s, recv_sem=r5r, device_id=sib, device_id_type=MESH,
    )
    give.start()
    mine_sum = term[rows_of(spot), :]
    first = wait_bytes(red, r1s, r1r)
    first.wait_recv()
    for n in range(7):
        mine_sum += red[n]
    line[cube] = mine_sum
    for n in FAR_FIRST:
        pltpu.make_async_remote_copy(
            src_ref=line.at[cube], dst_ref=line.at[cube],
            send_sem=r2s, recv_sem=r2r, device_id=(facing(n), core), device_id_type=MESH,
        ).start()

    give.wait_recv()

    @pl.loop(0, rows // 512)
    def _(b):
        at = pl.ds(pl.multiple_of(b * 512, 512), 512)
        total = sum(
            lax.dot_general(
                agg[h, at, :], wt[:, h * lanes : (h + 1) * lanes], (((1,), (1,)), ((), ())),
                preferred_element_type=jnp.float32,
            )
            for h in range(2)
        )
        ing[at, :] = total.astype(jnp.bfloat16)

    out_copy = pltpu.make_async_copy(ing, ing_hbm, out_sem.at[0])
    out_copy.start()
    second = wait_bytes(line.at[pl.ds(0, 7)], r2s, r2r)
    second.wait_recv()
    total = line[0]
    for n in range(1, 8):
        total += line[n]
    done[core, rows_of(spot), :] = total * jnp.float32(scale)
    def hand_out(to, send_sem, recv_sem):
        here = done.at[core, rows_of(spot)]
        pltpu.make_async_remote_copy(
            src_ref=here, dst_ref=here, send_sem=send_sem, recv_sem=recv_sem,
            device_id=to, device_id_type=MESH,
        ).start()

    for n in FAR_FIRST:
        hand_out((in_cube(n)[0], core), r3s, r3r)
        hand_out((in_cube(n)[0], 1 - core), r4s, r4r)
    hand_out(sib, r4s, r4r)
    for ph in range(2):
        wait_bytes(sbuf.at[ph, pl.ds(0, peers - 1)], ssem, ssem).wait_send()
        wait_bytes(sbuf.at[ph], fssem.at[ph], frsem.at[ph]).wait_send()
    for b in range(row_tiles // CHUNK):
        swap(b).wait_send()
    first.wait_send()
    second.wait_send()
    give.wait_send()
    third = wait_bytes(red, r3s, r3r)
    third.wait_recv()
    fourth = wait_bytes(line, r4s, r4r)
    mine_copy = pltpu.make_async_copy(done.at[core], wg_hbm.at[core], out_sem.at[1])
    mine_copy.start()
    third.wait_send()
    fourth.wait()
    sib_copy = pltpu.make_async_copy(done.at[1 - core], wg_hbm.at[1 - core], out_sem.at[2])
    sib_copy.start()
    out_copy.wait()
    mine_copy.wait()
    sib_copy.wait()


def finish_kernel(ing_in, wg_in, ing_out, wg_out, ing, wg, in_sem, out_sem):
    cuts = [
        (ing_in.at[at], ing.at[at], ing_out.at[at])
        for at in (pl.ds(n * 512, 512) for n in range(ing.shape[0] // 512))
    ]
    lanes = wg.shape[2]
    cuts += [
        (wg_in.at[h], wg.at[h], wg_out.at[:, pl.ds(h * lanes, lanes)]) for h in range(2)
    ]
    reads = [
        pltpu.make_async_copy(src, mid, in_sem.at[n])
        for n, (src, mid, _) in enumerate(cuts)
    ]
    writes = [
        pltpu.make_async_copy(mid, dst, out_sem.at[n])
        for n, (_, mid, dst) in enumerate(cuts)
    ]
    for read in reads:
        read.start()
    for read, write in zip(reads, writes):
        read.wait()
        write.start()
    for write in writes:
        write.wait()


def local(node_feats, out_grad, mask_bits, weight, send_rows, tile_vals, tile_row, tile_peer):
    rows, width = node_feats.shape
    peers, tile = send_rows.shape[1:]
    slots = tile_vals.shape[2]
    half = tile // 2
    row_tiles = rows // tile
    words = mask_bits.shape[1]
    most = -(-(slots + row_tiles * (GROUP - 1)) // GROUP)
    most = -(-most // UNROLL) * UNROLL
    places = -(-most * GROUP // 128) * 128
    piece = width // 8
    lanes = width // 2
    scale = 1.0 / math.sqrt(rows * lax.axis_size("row"))
    anywhere = pl.BlockSpec(memory_space=pl.ANY)
    bf16, f32, i32 = jnp.bfloat16, jnp.float32, jnp.int32
    dma = pltpu.SemaphoreType.DMA
    in_shape = jax.ShapeDtypeStruct((rows, width), bf16)
    parts = pl.pallas_call(
        lambda *refs: kernel(scale, *refs),
        out_shape=(in_shape, jax.ShapeDtypeStruct((2, width, lanes), f32)),
        in_specs=[anywhere] * 8,
        out_specs=(anywhere, anywhere),
        scratch_shapes=[
            pltpu.VMEM((rows, width), bf16),
            pltpu.VMEM((words, rows), i32),
            pltpu.VMEM((peers, tile), i32),
            pltpu.VMEM((1, slots), i32),
            pltpu.VMEM((1, slots), i32),
            pltpu.VMEM((rows, width), bf16),
            pltpu.VMEM((width, width), bf16),
            pltpu.VMEM((slots, tile, tile), bf16),
            pltpu.VMEM((rows, width), bf16),
            pltpu.VMEM((128, 128), i32),
            pltpu.VMEM((128, 128), i32),
            pltpu.VMEM((peers, half, 128), i32),
            pltpu.VMEM((4 * half, rows), bf16),
            pltpu.VMEM((2, peers, half // 2, width), bf16),
            pltpu.VMEM((peers + 1, half, width), bf16),
            pltpu.VMEM((peers + 1, half, width), bf16),
            pltpu.VMEM((8, places), i32),
            pltpu.SMEM((8, places), i32),
            pltpu.VMEM((most, tile, GROUP * half), bf16),
            pltpu.VMEM((most + 1, tile, width), f32),
            pltpu.VMEM((row_tiles, tile, width), f32),
            pltpu.VMEM((row_tiles, tile, lanes), f32),
            pltpu.VMEM((row_tiles, tile, lanes), f32),
            pltpu.VMEM((row_tiles, width, tile), bf16),
            pltpu.VMEM((rows, width), bf16),
            pltpu.VMEM((2, rows, lanes), bf16),
            pltpu.VMEM((width, lanes), f32),
            pltpu.VMEM((7, piece, lanes), f32),
            pltpu.VMEM((8, piece, lanes), f32),
            pltpu.VMEM((2, width, lanes), f32),
            dma((7,)), dma, dma, dma((2,)), dma((3,)),
            pltpu.SemaphoreType.REGULAR, dma, dma((16,)), dma((2,)), dma((2,)),
            dma((row_tiles // CHUNK,)), dma((row_tiles // CHUNK,)),
            dma, dma, dma, dma, dma, dma, dma, dma, dma, dma,
        ],
        compiler_params=pltpu.CompilerParams(
            collective_id=0, has_side_effects=True, vmem_limit_bytes=60 * 2**20
        ),
        name="layer",
    )(
        out_grad, mask_bits.T, send_rows[0], tile_row[0], tile_peer[0],
        node_feats, weight, tile_vals[0, 0],
    )
    return pl.pallas_call(
        finish_kernel,
        out_shape=(in_shape, jax.ShapeDtypeStruct((width, width), f32)),
        in_specs=[anywhere] * 2,
        out_specs=(anywhere, anywhere),
        scratch_shapes=[
            pltpu.VMEM((rows, width), bf16),
            pltpu.VMEM((2, width, lanes), f32),
            dma((rows // 512 + 2,)),
            dma((rows // 512 + 2,)),
        ],
        name="finish",
    )(*parts)


def solution(mesh):
    placed = (
        P("row", None),
        P("row", None),
        P("row", None),
        P(),
        P("row", None, None),
        P("row", "rep", None, None, None),
        P("row", "rep", None),
        P("row", "rep", None),
    )
    return jax.shard_map(
        local, mesh=mesh, in_specs=placed, out_specs=(P("row", None), P()), check_vma=False
    )
```
